32 devices in a mesh: groups: 2 (over y), node: 4 (over z), chip: 4 (over x, core).
Axes of the slice: x: 2, y: 2, z: 4, core: 2. Of those that a mesh axis runs over, the one named last changes fastest.
Arguments:
- tokens: bfloat16 [4096, 8192], P(('groups', 'node'), 'chip'), parts along dimension 0, may hold values from -6 to 6
- cotangent: bfloat16 [4096, 1024], P(('groups', 'node', 'chip')), parts along dimension 0, may hold values from -6 to 6
- frozen_value_weight: bfloat16 [8192, 1024], P('chip', 'node'), may hold values from -0.0625 to 0.0625
- adapter_a: bfloat16 [16, 8192, 64], P(('groups', 'node'), 'chip'), parts along dimension 0, may hold values from -0.0625 to 0.0625
- adapter_b: bfloat16 [16, 64, 1024], P(('groups', 'node'), 'chip'), parts along dimension 0, may hold values from -0.75 to 0.75
- first_a: float32 [16, 8192, 64], P(('groups', 'node'), 'chip'), parts along dimension 0, may hold values from -60 to 60
- first_b: float32 [16, 64, 1024], P(('groups', 'node'), 'chip'), parts along dimension 0, may hold values from -60 to 60
- second_a: float32 [16, 8192, 64], P(('groups', 'node'), 'chip'), parts along dimension 0, may hold values from 10 to 1000
- second_b: float32 [16, 64, 1024], P(('groups', 'node'), 'chip'), parts along dimension 0, may hold values from 10 to 1000
- token_slot: int32 [4096], P(('groups', 'node')), parts along dimension 0, may hold values from 0 to 1, as said below
- adapter_slot: int32 [16], P('groups'), parts along dimension 0, may hold values from 0 to 7, as said below
- request_list: int32 [8, 2], P(('groups', 'node')), parts along dimension 0, may hold values from 0 to 7, as said below
- request_count: int32 [8], P(('groups', 'node')), parts along dimension 0, may hold values from 1 to 2, as said below
Outputs:
- output: bfloat16 [4096, 1024], P(('groups', 'node', 'chip')), parts along dimension 0
- new_a: bfloat16 [16, 8192, 64], P(('groups', 'node'), 'chip'), parts along dimension 0
- new_b: bfloat16 [16, 64, 1024], P(('groups', 'node'), 'chip'), parts along dimension 0
- moment_a: float32 [16, 8192, 64], P(('groups', 'node'), 'chip'), parts along dimension 0
- moment_b: float32 [16, 64, 1024], P(('groups', 'node'), 'chip'), parts along dimension 0
- square_a: float32 [16, 8192, 64], P(('groups', 'node'), 'chip'), parts along dimension 0
- square_b: float32 [16, 64, 1024], P(('groups', 'node'), 'chip'), parts along dimension 0
The draws below stay inside these ranges and needn't reach their ends.
There are 2 independent parts, one for each index of `groups`. The reference program is written for one: setup_inputs(seed, part) draws one part's arguments, and reference() takes and returns one part's arrays. A program takes and returns all parts, laid end to end along the dimension named above; an argument that names none is the same for every part. Nothing has to cross between parts.
Inputs may be any that keep to these rules, and one draw needn't show every extreme that they name: `token_slot`: each token's position lies in 0 to 1; tokens at or past their node's count are padding. `adapter_slot`: A permutation of 0 to 7. `request_list`: the live entries of one node's list are distinct adapters with distinct owner nodes; entries past the count repeat live entries of the same list. `request_count`: some node has the full count and some other node the least count in every draw.
All inputs are finite; a program needn't handle non-finite values.
Results may differ from the reference program's by a relative error of at most 0.0045.
Values may be sent and summed in bfloat16 or wider, within the bound.
A program may use at most 128 MiB of HBM per device.

```python
import math
import jax
import jax.numpy as jnp
from jax import lax

D = 8192
KV = 1024
R = 64
ADP_NODE = 2
TOK_NODE = 512
ADAPTERS = 8
KMAX = 2
TOKENS = 2048
N_NODE = 4


def request_plan(key):
    base = jax.random.fold_in(key, 101)
    keys = jax.random.split(base, 7)
    order = jax.random.permutation(keys[0], ADAPTERS).astype(jnp.int32)
    popular = jax.random.randint(keys[1], (N_NODE,), 0, 4) * 2 ** 18
    scores = jax.random.randint(keys[2], (N_NODE, N_NODE), 0, 2 ** 18) + popular[None, :]
    scores = scores * N_NODE + jnp.arange(N_NODE, dtype=jnp.int32)[None, :]
    picked_scores, owners = lax.top_k(scores, KMAX)
    which = jax.random.randint(keys[3], (N_NODE, KMAX), 0, ADP_NODE)
    slots = owners.astype(jnp.int32) * ADP_NODE + which
    inverse = jnp.argsort(order).astype(jnp.int32)
    ids = jnp.take(inverse, slots, axis=0)
    lowest = KMAX // 2
    counts = jax.random.randint(keys[4], (N_NODE,), lowest, KMAX + 1)
    full_node = jax.random.randint(keys[5], (), 0, N_NODE)
    low_step = jax.random.randint(keys[6], (), 1, N_NODE)
    low_node = (full_node + low_step) % N_NODE
    counts = counts.at[full_node].set(KMAX)
    counts = counts.at[low_node].set(lowest).astype(jnp.int32)
    positions = jnp.arange(KMAX, dtype=jnp.int32)
    source = jnp.where(positions[None, :] < counts[:, None], positions[None, :], positions[None, :] - counts[:, None])
    ids = jnp.take_along_axis(ids, source, axis=1).astype(jnp.int32)
    return (order, ids, counts)


def draw_adapter_slot(key, part):
    order, ids, counts = request_plan(key)
    return order


def draw_request_list(key, part):
    order, ids, counts = request_plan(key)
    return ids


def draw_request_count(key, part):
    order, ids, counts = request_plan(key)
    return counts


def draw_token_slot(key, part):
    key = jax.random.fold_in(key, 7)
    return jax.random.randint(key, (TOKENS,), 0, KMAX).astype(jnp.int32)


def block_levels(stream_key, dims, cuts, smallest, top_value):
    factor_of, own = 1.0, jax.random.fold_in(stream_key, 6)
    for position, blocks in cuts:
        heights = jnp.exp(jax.random.uniform(jax.random.fold_in(own, position), (blocks,), jnp.float32, smallest / len(cuts), top_value / len(cuts)))
        factor_of = factor_of * jnp.repeat(heights, dims[position] // blocks).reshape([-1 if axis == position else 1 for axis in range(len(dims))])
    return factor_of


def gaussian(own_key, dims, deviation, limit, cuts=(), kind=jnp.bfloat16):
    array = deviation * jax.random.normal(own_key, dims, jnp.float32)
    if cuts:
        array = array * block_levels(own_key, dims, cuts, -0.22, 0.18)
    return jnp.clip(array, -limit, limit).astype(kind)


def setup_inputs(seed: int = 0, part: int = 0) -> dict:
    arg_keys = jax.random.split(jax.random.key(seed), 14)
    part_splits = jax.random.split(jax.random.fold_in(arg_keys[13], part), 14)
    return {
        "tokens": gaussian(part_splits[0], (TOKENS, D), 1.0, 6.0, ((0, 4), (1, 4))),
        "cotangent": gaussian(part_splits[1], (TOKENS, KV), 1.0, 6.0, ((0, 16),)),
        "frozen_value_weight": gaussian(arg_keys[2], (D, KV), D ** -0.5, 0.0625, ((0, 4), (1, 4))),
        "adapter_a": gaussian(part_splits[3], (ADAPTERS, D, R), D ** -0.5, 0.0625, ((0, 4), (1, 4))),
        "adapter_b": gaussian(part_splits[4], (ADAPTERS, R, KV), R ** -0.5, 0.75, ((0, 4), (1, 4))),
        "first_a": gaussian(part_splits[5], (ADAPTERS, D, R), 10.0, 60.0, ((0, 4), (1, 4)), jnp.float32),
        "first_b": gaussian(part_splits[6], (ADAPTERS, R, KV), 10.0, 60.0, ((0, 4), (1, 4)), jnp.float32),
        "second_a": jnp.clip(jnp.exp(math.log(1000.0) - 4.6051702 * jax.random.uniform(part_splits[7], (ADAPTERS, D, R), jnp.float32) ** block_levels(part_splits[7], (ADAPTERS, D, R), ((0, 4), (1, 4)), -0.2, 0.2)), 10.0, 1000.0),
        "second_b": jnp.clip(jnp.exp(math.log(1000.0) - 4.6051702 * jax.random.uniform(part_splits[8], (ADAPTERS, R, KV), jnp.float32) ** block_levels(part_splits[8], (ADAPTERS, R, KV), ((0, 4), (1, 4)), -0.2, 0.2)), 10.0, 1000.0),
        "token_slot": draw_token_slot(jax.random.fold_in(jax.random.fold_in(arg_keys[13], part), 71), part),
        "adapter_slot": draw_adapter_slot(jax.random.fold_in(jax.random.fold_in(arg_keys[13], part), 71), part),
        "request_list": draw_request_list(jax.random.fold_in(jax.random.fold_in(arg_keys[13], part), 71), part),
        "request_count": draw_request_count(jax.random.fold_in(jax.random.fold_in(arg_keys[13], part), 71), part),
    }


adapter_scale = 2.0
beta_one = 0.9
beta_two = 0.999
rate = 0.001
eps_adam = 1e-08
bias_one = 1.0
bias_two = 0.632304575229036

def adam_update(param, first, second, grad):
    first_new = beta_one * first + (1.0 - beta_one) * grad
    second_new = beta_two * second + (1.0 - beta_two) * grad * grad
    update = first_new / bias_one / (jnp.sqrt(second_new / bias_two) + eps_adam)
    return ((param.astype(jnp.float32) - rate * update).astype(jnp.bfloat16), first_new, second_new)

def reference(tokens, cotangent, frozen_value_weight, adapter_a, adapter_b, first_a, first_b, second_a, second_b, token_slot, adapter_slot, request_list, request_count):
    x_nodes = tokens.reshape(N_NODE, TOK_NODE, D)
    cot_nodes = cotangent.reshape(N_NODE, TOK_NODE, KV)
    slot_nodes = token_slot.reshape(N_NODE, TOK_NODE)
    positions = jnp.arange(KMAX, dtype=jnp.int32)

    def per_node(carry, item):
        grad_a, grad_b = carry
        input_rows, cot_rows, slots, ids, count = item
        rows = jnp.take(adapter_slot, ids, axis=0).astype(jnp.int32)
        live = positions < count
        onehot = ((slots[:, None] == positions[None, :]) & live[None, :]).astype(jnp.float32)
        mats_a = jnp.take(adapter_a, rows, axis=0).astype(jnp.float32)
        second_matrices = jnp.take(adapter_b, rows, axis=0).astype(jnp.float32)
        inputs_f = input_rows.astype(jnp.float32)
        cotangent_wide = cot_rows.astype(jnp.float32)
        low_all = jnp.einsum('td,kdr->tkr', inputs_f, mats_a)
        low = jnp.einsum('tkr,tk->tr', low_all, onehot, precision=lax.Precision.HIGHEST)
        low_bf = low.astype(jnp.bfloat16).astype(jnp.float32)
        spread_rows = onehot[:, :, None] * low_bf[:, None, :]
        low_rank_delta = jnp.einsum('web,ebs->ws', spread_rows, second_matrices)
        final_output = jnp.dot(input_rows, frozen_value_weight, preferred_element_type=jnp.float32) + adapter_scale * low_rank_delta
        back_all = jnp.einsum('tv,krv->tkr', cotangent_wide, second_matrices)
        backward_rows = jnp.einsum('tkr,tk->tr', back_all, onehot, precision=lax.Precision.HIGHEST)
        backward_half_width = (adapter_scale * backward_rows).astype(jnp.bfloat16).astype(jnp.float32)
        spread_back = onehot[:, :, None] * backward_half_width[:, None, :]
        part_a = jnp.einsum('td,tkr->kdr', inputs_f, spread_back)
        second_partial = adapter_scale * jnp.einsum('cwy,cs->wys', spread_rows, cotangent_wide)
        grad_a = grad_a.at[rows].add(part_a)
        grad_b = grad_b.at[rows].add(second_partial)
        return ((grad_a, grad_b), final_output.astype(jnp.bfloat16))
    start = (jnp.zeros((ADAPTERS, D, R), jnp.float32), jnp.zeros((ADAPTERS, R, KV), jnp.float32))
    (grad_a, grad_b), results = lax.scan(per_node, start, (x_nodes, cot_nodes, slot_nodes, request_list, request_count))
    output = results.reshape(TOKENS, KV)
    new_a, moment_a, square_a = adam_update(adapter_a, first_a, second_a, grad_a)
    new_b, moment_b, square_b = adam_update(adapter_b, first_b, second_b, grad_b)
    return (output, new_a, new_b, moment_a, moment_b, square_a, square_b)
```

```python
import functools

import jax
import jax.numpy as jnp
from jax import lax
from jax.experimental import pallas as pl
from jax.experimental.pallas import tpu as pltpu
from jax.sharding import PartitionSpec as P

adapter_scale = 2.0
beta_one = 0.9
beta_two = 0.999
rate = 0.001
eps_adam = 1e-08
bias_one = 1.0
bias_two = 0.632304575229036


def adam_update(param, first, second, grad):
    first_new = beta_one * first + (1.0 - beta_one) * grad
    second_new = beta_two * second + (1.0 - beta_two) * grad * grad
    update = first_new / bias_one / (jnp.sqrt(second_new / bias_two) + eps_adam)
    return ((param.astype(jnp.float32) - rate * update).astype(jnp.bfloat16), first_new, second_new)


def local_plain(
    tokens,
    cotangent,
    frozen_value_weight,
    adapter_a,
    adapter_b,
    first_a,
    first_b,
    second_a,
    second_b,
    token_slot,
    adapter_slot,
    request_list,
    request_count,
):
    nodes = lax.axis_size("node")
    this_node = lax.axis_index("node")
    this_chip = lax.axis_index("chip")
    owned = adapter_a.shape[0]
    most = request_list.shape[1]
    rank_part = adapter_b.shape[1]
    width_out = adapter_b.shape[2]
    rows_here = tokens.shape[0]
    positions = jnp.arange(most, dtype=jnp.int32)
    owner_ids = jnp.arange(nodes, dtype=jnp.int32)
    local_ids = jnp.arange(owned, dtype=jnp.int32)
    my_rows = jnp.take(adapter_slot, request_list[0], axis=0)
    my_owner = my_rows // owned
    my_valid = positions < request_count[0]
    all_lists, all_counts = (
        lax.all_gather(request_list, "node", axis=0, tiled=True),
        lax.all_gather(request_count, "node", axis=0, tiled=True),
    )
    all_rows = jnp.take(adapter_slot, all_lists, axis=0)
    hits = (positions[None, :] < all_counts[:, None]) & (all_rows // owned == this_node)
    picks = jnp.sum(
        (hits[:, :, None] & ((all_rows % owned)[:, :, None] == local_ids[None, None, :])).astype(
            jnp.float32
        ),
        axis=1,
    )
    picks_low = picks.astype(jnp.bfloat16)
    send_a = jnp.einsum(
        "pj,jdr->pdr", picks_low, adapter_a, preferred_element_type=jnp.float32
    ).astype(jnp.bfloat16)
    send_b = jnp.einsum(
        "pj,jrv->prv", picks_low, adapter_b, preferred_element_type=jnp.float32
    ).astype(jnp.bfloat16)
    recv_a, recv_b = (
        lax.all_to_all(send_a, "node", split_axis=0, concat_axis=0, tiled=True),
        lax.all_to_all(send_b, "node", split_axis=0, concat_axis=0, tiled=True),
    )
    fetched_a = jnp.take(recv_a, my_owner, axis=0)
    fetched_b = jnp.take(recv_b, my_owner, axis=0)
    onehot = (token_slot[:, None] == positions[None, :]) & my_valid[None, :]
    onehot_f = onehot.astype(jnp.float32)
    onehot_b = onehot.astype(jnp.bfloat16)
    low_part = jnp.einsum("td,kdr->tkr", tokens, fetched_a, preferred_element_type=jnp.float32)
    low_sel = jnp.einsum("tkr,tk->tr", low_part, onehot_f, precision=lax.Precision.HIGHEST)
    low_rank = lax.psum(low_sel, "chip")
    low_bf = low_rank.astype(jnp.bfloat16)
    low_mine = lax.dynamic_slice_in_dim(low_bf, this_chip * rank_part, rank_part, 1)
    spread_rows = (onehot_b[:, :, None] * low_mine[:, None, :]).reshape(rows_here, most * rank_part)
    up_flattened = fetched_b.reshape(most * rank_part, width_out)
    frozen_output = jnp.dot(
        tokens,
        lax.all_gather(frozen_value_weight, "node", axis=1, tiled=True),
        preferred_element_type=jnp.float32,
    )
    partial_terms = frozen_output + adapter_scale * jnp.dot(
        spread_rows, up_flattened, preferred_element_type=jnp.float32
    )
    output = lax.psum_scatter(partial_terms, "chip", scatter_dimension=0, tiled=True).astype(
        jnp.bfloat16
    )
    cot_whole = lax.all_gather(cotangent, "chip", axis=0, tiled=True)
    back_part = jnp.einsum("tv,krv->tkr", cot_whole, fetched_b, preferred_element_type=jnp.float32)
    backward_selected = jnp.einsum(
        "tkr,tk->tr", back_part, onehot_f, precision=lax.Precision.HIGHEST
    )
    backward_half_width = (adapter_scale * backward_selected).astype(jnp.bfloat16)
    back_rank = lax.all_gather(backward_half_width, "chip", axis=1, tiled=True)
    spread_back = onehot_b[:, :, None] * back_rank[:, None, :]
    grad_down = jnp.einsum("td,tkr->kdr", tokens, spread_back, preferred_element_type=jnp.float32)
    up_gradient = adapter_scale * jnp.einsum(
        "tk,tv->kv", spread_rows, cot_whole, preferred_element_type=jnp.float32
    )
    up_gradient = up_gradient.reshape(most, rank_part, width_out)
    route = (my_valid[:, None] & (my_owner[:, None] == owner_ids[None, :])).astype(jnp.float32)
    send_down = jnp.einsum("ko,kdr->odr", route, grad_down, precision=lax.Precision.HIGHEST)
    send_up = jnp.einsum("ko,krv->orv", route, up_gradient, precision=lax.Precision.HIGHEST)
    recv_down, recv_up = (
        lax.all_to_all(
            send_down.astype(jnp.bfloat16), "node", split_axis=0, concat_axis=0, tiled=True
        ).astype(send_down.dtype),
        lax.all_to_all(
            send_up.astype(jnp.bfloat16), "node", split_axis=0, concat_axis=0, tiled=True
        ).astype(send_up.dtype),
    )
    total_down = jnp.einsum("pj,pdr->jdr", picks, recv_down, precision=lax.Precision.HIGHEST)
    total_up = jnp.einsum("pj,prv->jrv", picks, recv_up, precision=lax.Precision.HIGHEST)
    new_a, moment_a, square_a = adam_update(adapter_a, first_a, second_a, total_down)
    new_b, moment_b, square_b = adam_update(adapter_b, first_b, second_b, total_up)
    return (output, new_a, new_b, moment_a, moment_b, square_a, square_b)


MESH = pl.DeviceIdType.MESH
NT = (((1,), (1,)), ((), ()))
TN = (((0,), (0,)), ((), ()))
F32 = jnp.float32
BF16 = jnp.bfloat16


def rows_of(index, size):
    return pl.ds(pl.multiple_of(index * size, size), size)


def step_kernel(
    nodes,
    chips,
    groups,
    slot_ref,
    list_ref,
    count_ref,
    token_slot_ref,
    tokens_ref,
    cot_ref,
    w_ref,
    a_ref,
    b_ref,
    out_ref,
    total_a_ref,
    total_b_ref,
    info,
    cot_all,
    w_all,
    send_a,
    recv_a,
    send_b,
    recv_b,
    back_all,
    grad_a,
    got_a,
    grad_b,
    got_b,
    low_all,
    low_send,
    low_recv,
    lora,
    part_send,
    part_recv,
    info_sem,
    cot_sem,
    a_sem,
    b_sem,
    back_sem,
    low_sem,
    ga_sem,
    gb_sem,
    w_sem,
    wg_send_sem,
    wg_recv_sem,
    part_send_sem,
    part_recv_sem,
):
    me = lax.axis_index("node")
    chip = lax.axis_index("chip")
    group = lax.axis_index("groups")
    owned, rank, depth = a_ref.shape
    rank_part = b_ref.shape[1]
    most = list_ref.shape[1]
    tokens_n = tokens_ref.shape[0]
    out_rows, width = cot_ref.shape
    w_cols = w_ref.shape[1]
    half = depth // groups

    barrier = pltpu.get_barrier_semaphore()
    for axis, size, here in (("node", nodes, me), ("chip", chips, chip), ("groups", groups, group)):
        for o in range(1, size):
            pl.semaphore_signal(
                barrier, inc=1, device_id={axis: lax.rem(here + o, size)}, device_id_type=MESH
            )

    lane = lax.broadcasted_iota(jnp.int32, (8, 128), 1)
    mine = jnp.full((8, 128), -1, jnp.int32)
    slots = token_slot_ref[...]
    tok_row = jnp.full(slots.shape, -1, jnp.int32)
    for k in range(most):
        row = jnp.where(k < count_ref[0], slot_ref[list_ref[0, k]], -1)
        mine = jnp.where(lane == k, row, mine)
        tok_row = jnp.where(slots == k, row, tok_row)
    info[me] = mine
    masks = [
        jnp.where((tok_row >= p * owned) & (tok_row < (p + 1) * owned), 1.0, 0.0).astype(F32)
        for p in range(nodes)
    ]
    pl.semaphore_wait(barrier, nodes + chips + groups - 3)

    def exchange(axis, size, here, sem, src_of, dst):
        copies = []
        for o in range(1, size):
            peer = lax.rem(here + o, size)
            copies.append(
                pltpu.make_async_remote_copy(
                    src_ref=src_of(peer),
                    dst_ref=dst,
                    send_sem=sem.at[0, o - 1],
                    recv_sem=sem.at[1, o - 1],
                    device_id={axis: peer},
                    device_id_type=MESH,
                )
            )
        return copies

    def start(copies):
        for c in copies:
            c.start()

    def landed(copies):
        for c in copies:
            c.wait_recv()

    info_copies = exchange("node", nodes, me, info_sem, lambda q: info.at[me], info.at[me])
    start(info_copies)
    cot_copies = exchange(
        "chip", chips, chip, cot_sem, lambda q: cot_ref, cot_all.at[rows_of(chip, out_rows)]
    )
    start(cot_copies)

    my_half = rows_of(group, half)

    def w_hop(way, j):
        shard = me - j if way == 0 else me + j
        have = (shard >= 0) if way == 0 else (shard < nodes)
        may = (me < nodes - 1) if way == 0 else (me > 0)
        peer = me + 1 if way == 0 else me - 1
        src = w_ref.at[my_half] if j == 0 else w_all.at[shard, my_half]
        copy = pltpu.make_async_remote_copy(
            src_ref=src,
            dst_ref=w_all.at[shard, my_half],
            send_sem=w_sem.at[0, way, j],
            recv_sem=w_sem.at[1, way, j],
            device_id={"node": peer},
            device_id_type=MESH,
        )
        return have & may, copy

    def w_from(way, j):
        shard = me - 1 - j if way == 0 else me + 1 + j
        have = (shard >= 0) if way == 0 else (shard < nodes)
        return have, shard

    def w_share(way, j, shard):
        copies = []
        for o in range(1, groups):
            copies.append(
                pltpu.make_async_remote_copy(
                    src_ref=w_all.at[shard, my_half],
                    dst_ref=w_all.at[shard, my_half],
                    send_sem=wg_send_sem.at[way, j, o - 1],
                    recv_sem=wg_recv_sem.at[way, j, o - 1],
                    device_id={"groups": lax.rem(group + o, groups)},
                    device_id_type=MESH,
                )
            )
        return copies

    def w_send(way, j):
        go, copy = w_hop(way, j)

        @pl.when(go)
        def _():
            copy.start()

    def w_step(j):
        for way in (0, 1):
            have, shard = w_from(way, j)

            @pl.when(have)
            def _():
                pltpu.make_async_remote_copy(
                    src_ref=w_all.at[shard, my_half],
                    dst_ref=w_all.at[shard, my_half],
                    send_sem=w_sem.at[0, way, j],
                    recv_sem=w_sem.at[1, way, j],
                    device_id={"node": me - 1 if way == 0 else me + 1},
                    device_id_type=MESH,
                ).wait_recv()
                start(w_share(way, j, shard))

            if j + 1 < nodes - 1:
                w_send(way, j + 1)

    w_send(0, 0)
    w_send(1, 0)
    cot_all[rows_of(chip, out_rows), :] = cot_ref[...]

    landed(info_copies)

    def picks(q):
        found = info[q]
        return [
            jnp.max(jnp.where(found == me * owned + j, 1.0, 0.0).astype(F32)) for j in range(owned)
        ]

    b_copies = exchange(
        "node",
        nodes,
        me,
        b_sem,
        lambda q: send_b.at[rows_of(q, rank_part)],
        recv_b.at[rows_of(me, rank_part)],
    )
    a_copies = exchange(
        "node", nodes, me, a_sem, lambda q: send_a.at[rows_of(q, rank)], recv_a.at[rows_of(me, rank)]
    )
    for o in range(1, nodes + 1):
        q = lax.rem(me + o, nodes)
        pick = picks(q)
        chosen = sum(pick[j] * b_ref[j].astype(F32) for j in range(owned)).astype(BF16)
        if o < nodes:
            send_b[rows_of(q, rank_part), :] = chosen
            b_copies[o - 1].start()
        else:
            recv_b[rows_of(me, rank_part), :] = chosen
    for o in range(1, nodes + 1):
        q = lax.rem(me + o, nodes)
        pick = picks(q)
        chosen = sum(pick[j] * a_ref[j].astype(F32) for j in range(owned)).astype(BF16)
        if o < nodes:
            send_a[rows_of(q, rank), :] = chosen
            a_copies[o - 1].start()
        else:
            recv_a[rows_of(me, rank), :] = chosen

    landed(cot_copies)
    landed(b_copies)
    every = lax.dot_general(recv_b[...], cot_all[...], NT, preferred_element_type=F32)
    back = sum(
        masks[p] * every[p * rank_part : (p + 1) * rank_part] for p in range(nodes)
    )
    back_all[rows_of(chip, rank_part), :] = (adapter_scale * back).astype(BF16)
    back_copies = exchange(
        "chip",
        chips,
        chip,
        back_sem,
        lambda q: back_all.at[rows_of(chip, rank_part)],
        back_all.at[rows_of(chip, rank_part)],
    )
    start(back_copies)
    w_step(0)
    landed(back_copies)

    whole_back = back_all[...].astype(F32)
    spread_back = jnp.concatenate([masks[p] * whole_back for p in range(nodes)], axis=0).astype(BF16)
    tile = min(512, depth)
    for t in range(depth // tile):
        cols = slice(t * tile, (t + 1) * tile)
        grad_a[:, cols] = jnp.dot(
            spread_back, tokens_ref[:, cols], preferred_element_type=F32
        ).astype(BF16)
    ga_copies = exchange(
        "node", nodes, me, ga_sem, lambda q: grad_a.at[rows_of(q, rank)], got_a.at[rows_of(me, rank)]
    )
    start(ga_copies)
    got_a[rows_of(me, rank), :] = grad_a[rows_of(me, rank), :]

    if nodes > 2:
        w_step(1)

    landed(a_copies)
    low_all[...] = lax.dot_general(
        recv_a[...], tokens_ref[...], NT, preferred_element_type=F32
    )
    low_send[...] = sum(masks[p] * low_all[p * rank : (p + 1) * rank, :] for p in range(nodes))
    low_copies = exchange(
        "chip",
        chips,
        chip,
        low_sem,
        lambda q: low_send.at[rows_of(q, rank_part)],
        low_recv.at[chip],
    )
    start(low_copies)
    low_recv[chip] = low_send[rows_of(chip, rank_part), :]
    landed(low_copies)
    low_mine = sum(low_recv[c] for c in range(chips)).astype(BF16).astype(F32)
    spread_low = jnp.concatenate([masks[p] * low_mine for p in range(nodes)], axis=0).astype(BF16)
    grad_b[...] = (
        adapter_scale * jnp.dot(spread_low, cot_all[...], preferred_element_type=F32)
    ).astype(BF16)
    gb_copies = exchange(
        "node",
        nodes,
        me,
        gb_sem,
        lambda q: grad_b.at[rows_of(q, rank_part)],
        got_b.at[rows_of(me, rank_part)],
    )
    start(gb_copies)
    got_b[rows_of(me, rank_part), :] = grad_b[rows_of(me, rank_part), :]
    lora[...] = adapter_scale * lax.dot_general(
        spread_low, recv_b[...], TN, preferred_element_type=F32
    )

    def part_copies(shard):
        copies = []
        cols = rows_of(shard, w_cols)
        for o in range(1, chips):
            peer = lax.rem(chip + o, chips)
            copies.append(
                pltpu.make_async_remote_copy(
                    src_ref=part_send.at[rows_of(peer, out_rows), cols],
                    dst_ref=part_recv.at[chip, :, cols],
                    send_sem=part_send_sem.at[shard, o - 1],
                    recv_sem=part_recv_sem.at[shard, o - 1],
                    device_id={"chip": peer},
                    device_id_type=MESH,
                )
            )
        return copies

    def chunk(shard, weight):
        cols = rows_of(shard, w_cols)

        def body(c, carry):
            rows = rows_of(c, out_rows)
            part_send[rows, cols] = (
                jnp.dot(tokens_ref[rows, :], weight[...], preferred_element_type=F32)
                + lora[rows, cols]
            ).astype(BF16)
            return carry

        lax.fori_loop(0, chips, body, 0)
        start(part_copies(shard))

    chunk(me, w_ref)
    for j in range(nodes - 1):
        if j >= 2:
            w_step(j)
        for way in (0, 1):
            have, shard = w_from(way, j)

            @pl.when(have)
            def _():
                for o in range(1, groups):
                    theirs = rows_of(lax.rem(group + groups - o, groups), half)
                    pltpu.make_async_remote_copy(
                        src_ref=w_all.at[shard, theirs],
                        dst_ref=w_all.at[shard, theirs],
                        send_sem=wg_send_sem.at[way, j, o - 1],
                        recv_sem=wg_recv_sem.at[way, j, o - 1],
                        device_id={"groups": lax.rem(group + o, groups)},
                        device_id_type=MESH,
                    ).wait_recv()
                chunk(shard, w_all.at[shard])

    landed(ga_copies)
    landed(gb_copies)
    weights = [picks(q) for q in range(nodes)]
    for j in range(owned):
        total_a_ref[j] = sum(
            weights[q][j] * got_a[q * rank : (q + 1) * rank, :].astype(F32) for q in range(nodes)
        )
        total_b_ref[j] = sum(
            weights[q][j] * got_b[q * rank_part : (q + 1) * rank_part, :].astype(F32)
            for q in range(nodes)
        )

    for shard in range(nodes):
        landed(part_copies(shard))
    part_recv[chip] = part_send[rows_of(chip, out_rows), :]
    out_ref[...] = sum(part_recv[c].astype(F32) for c in range(chips)).astype(BF16)

    for copies in (
        info_copies,
        cot_copies,
        b_copies,
        a_copies,
        back_copies,
        ga_copies,
        low_copies,
        gb_copies,
    ):
        for c in copies:
            c.wait_send()
    for shard in range(nodes):
        for c in part_copies(shard):
            c.wait_send()
    for j in range(nodes - 1):
        for way in (0, 1):
            go, copy = w_hop(way, j)

            @pl.when(go)
            def _():
                copy.wait_send()

            have, shard = w_from(way, j)

            @pl.when(have)
            def _():
                for c in w_share(way, j, shard):
                    c.wait_send()


def local_fused(
    nodes,
    chips,
    groups,
    tokens,
    cotangent,
    frozen_value_weight,
    adapter_a,
    adapter_b,
    first_a,
    first_b,
    second_a,
    second_b,
    token_slot,
    adapter_slot,
    request_list,
    request_count,
):
    owned, depth, rank = adapter_a.shape
    rank_part = adapter_b.shape[1]
    rows = tokens.shape[0]
    out_rows, width = cotangent.shape
    w_cols = frozen_value_weight.shape[1]
    vmem = pl.BlockSpec(memory_space=pltpu.VMEM)
    smem = pl.BlockSpec(memory_space=pltpu.SMEM)
    dma = pltpu.SemaphoreType.DMA
    output, total_a, total_b = pl.pallas_call(
        functools.partial(step_kernel, nodes, chips, groups),
        out_shape=(
            jax.ShapeDtypeStruct((out_rows, width), BF16),
            jax.ShapeDtypeStruct((owned, rank, depth), F32),
            jax.ShapeDtypeStruct((owned, rank_part, width), F32),
        ),
        in_specs=[smem] * 3 + [vmem] * 6,
        out_specs=(vmem, vmem, vmem),
        scratch_shapes=[
            pltpu.VMEM((nodes, 8, 128), jnp.int32),
            pltpu.VMEM((rows, width), BF16),
            pltpu.VMEM((nodes, depth, w_cols), BF16),
            pltpu.VMEM((nodes * rank, depth), BF16),
            pltpu.VMEM((nodes * rank, depth), BF16),
            pltpu.VMEM((nodes * rank_part, width), BF16),
            pltpu.VMEM((nodes * rank_part, width), BF16),
            pltpu.VMEM((rank, rows), BF16),
            pltpu.VMEM((nodes * rank, depth), BF16),
            pltpu.VMEM((nodes * rank, depth), BF16),
            pltpu.VMEM((nodes * rank_part, width), BF16),
            pltpu.VMEM((nodes * rank_part, width), BF16),
            pltpu.VMEM((nodes * rank, rows), F32),
            pltpu.VMEM((rank, rows), F32),
            pltpu.VMEM((chips, rank_part, rows), F32),
            pltpu.VMEM((rows, width), F32),
            pltpu.VMEM((rows, width), BF16),
            pltpu.VMEM((chips, out_rows, width), BF16),
            dma((2, nodes - 1)),
            dma((2, chips - 1)),
            dma((2, nodes - 1)),
            dma((2, nodes - 1)),
            dma((2, chips - 1)),
            dma((2, chips - 1)),
            dma((2, nodes - 1)),
            dma((2, nodes - 1)),
            dma((2, 2, nodes - 1)),
            dma((2, nodes - 1, groups - 1)),
            dma((2, nodes - 1, groups - 1)),
            dma((nodes, chips - 1)),
            dma((nodes, chips - 1)),
        ],
        compiler_params=pltpu.CompilerParams(
            collective_id=0, has_side_effects=True, vmem_limit_bytes=48 * 1024 * 1024
        ),
        cost_estimate=pl.CostEstimate(
            flops=2 * rows * depth * (width + 2 * nodes * rank),
            bytes_accessed=8 * 1024 * 1024,
            transcendentals=0,
        ),
    )(
        adapter_slot,
        request_list,
        request_count,
        token_slot.reshape(1, rows),
        tokens,
        cotangent,
        frozen_value_weight,
        jnp.swapaxes(adapter_a, 1, 2),
        adapter_b,
    )
    new_a, moment_a, square_a = adam_update(
        adapter_a, first_a, second_a, jnp.swapaxes(total_a, 1, 2)
    )
    new_b, moment_b, square_b = adam_update(adapter_b, first_b, second_b, total_b)
    return (output, new_a, new_b, moment_a, moment_b, square_a, square_b)


def solution(mesh):
    nodes, chips, groups = (mesh.shape[name] for name in ("node", "chip", "groups"))
    fits = 2 <= nodes <= 4 and chips >= 2 and groups >= 2
    local = functools.partial(local_fused, nodes, chips, groups) if fits else local_plain
    return jax.shard_map(
        local,
        mesh=mesh,
        in_specs=(
            P(("groups", "node"), "chip"),
            P(("groups", "node", "chip"), None),
            P("chip", "node"),
            P(("groups", "node"), "chip", None),
            P(("groups", "node"), "chip", None),
            P(("groups", "node"), "chip", None),
            P(("groups", "node"), "chip", None),
            P(("groups", "node"), "chip", None),
            P(("groups", "node"), "chip", None),
            P(("groups", "node")),
            P("groups"),
            P(("groups", "node"), None),
            P(("groups", "node")),
        ),
        out_specs=(
            P(("groups", "node", "chip"), None),
            P(("groups", "node"), "chip", None),
            P(("groups", "node"), "chip", None),
            P(("groups", "node"), "chip", None),
            P(("groups", "node"), "chip", None),
            P(("groups", "node"), "chip", None),
            P(("groups", "node"), "chip", None),
        ),
        check_vma=False,
    )
```

```python
import functools

import jax
import jax.numpy as jnp
from jax import lax
from jax.experimental import pallas as pl
from jax.experimental.pallas import tpu as pltpu
from jax.sharding import PartitionSpec as P

adapter_scale = 2.0
beta_one = 0.9
beta_two = 0.999
rate = 0.001
eps_adam = 1e-08
bias_one = 1.0
bias_two = 0.632304575229036


def adam_update(param, first, second, grad):
    first_new = beta_one * first + (1.0 - beta_one) * grad
    second_new = beta_two * second + (1.0 - beta_two) * grad * grad
    update = first_new / bias_one / (jnp.sqrt(second_new / bias_two) + eps_adam)
    return ((param.astype(jnp.float32) - rate * update).astype(jnp.bfloat16), first_new, second_new)


def local_plain(
    tokens,
    cotangent,
    frozen_value_weight,
    adapter_a,
    adapter_b,
    first_a,
    first_b,
    second_a,
    second_b,
    token_slot,
    adapter_slot,
    request_list,
    request_count,
):
    nodes = lax.axis_size("node")
    this_node = lax.axis_index("node")
    this_chip = lax.axis_index("chip")
    owned = adapter_a.shape[0]
    most = request_list.shape[1]
    rank_part = adapter_b.shape[1]
    width_out = adapter_b.shape[2]
    rows_here = tokens.shape[0]
    positions = jnp.arange(most, dtype=jnp.int32)
    owner_ids = jnp.arange(nodes, dtype=jnp.int32)
    local_ids = jnp.arange(owned, dtype=jnp.int32)
    my_rows = jnp.take(adapter_slot, request_list[0], axis=0)
    my_owner = my_rows // owned
    my_valid = positions < request_count[0]
    all_lists, all_counts = (
        lax.all_gather(request_list, "node", axis=0, tiled=True),
        lax.all_gather(request_count, "node", axis=0, tiled=True),
    )
    all_rows = jnp.take(adapter_slot, all_lists, axis=0)
    hits = (positions[None, :] < all_counts[:, None]) & (all_rows // owned == this_node)
    picks = jnp.sum(
        (hits[:, :, None] & ((all_rows % owned)[:, :, None] == local_ids[None, None, :])).astype(
            jnp.float32
        ),
        axis=1,
    )
    picks_low = picks.astype(jnp.bfloat16)
    send_a = jnp.einsum(
        "pj,jdr->pdr", picks_low, adapter_a, preferred_element_type=jnp.float32
    ).astype(jnp.bfloat16)
    send_b = jnp.einsum(
        "pj,jrv->prv", picks_low, adapter_b, preferred_element_type=jnp.float32
    ).astype(jnp.bfloat16)
    recv_a, recv_b = (
        lax.all_to_all(send_a, "node", split_axis=0, concat_axis=0, tiled=True),
        lax.all_to_all(send_b, "node", split_axis=0, concat_axis=0, tiled=True),
    )
    fetched_a = jnp.take(recv_a, my_owner, axis=0)
    fetched_b = jnp.take(recv_b, my_owner, axis=0)
    onehot = (token_slot[:, None] == positions[None, :]) & my_valid[None, :]
    onehot_f = onehot.astype(jnp.float32)
    onehot_b = onehot.astype(jnp.bfloat16)
    low_part = jnp.einsum("td,kdr->tkr", tokens, fetched_a, preferred_element_type=jnp.float32)
    low_sel = jnp.einsum("tkr,tk->tr", low_part, onehot_f, precision=lax.Precision.HIGHEST)
    low_rank = lax.psum(low_sel, "chip")
    low_bf = low_rank.astype(jnp.bfloat16)
    low_mine = lax.dynamic_slice_in_dim(low_bf, this_chip * rank_part, rank_part, 1)
    spread_rows = (onehot_b[:, :, None] * low_mine[:, None, :]).reshape(rows_here, most * rank_part)
    up_flattened = fetched_b.reshape(most * rank_part, width_out)
    frozen_output = jnp.dot(
        tokens,
        lax.all_gather(frozen_value_weight, "node", axis=1, tiled=True),
        preferred_element_type=jnp.float32,
    )
    partial_terms = frozen_output + adapter_scale * jnp.dot(
        spread_rows, up_flattened, preferred_element_type=jnp.float32
    )
    output = lax.psum_scatter(partial_terms, "chip", scatter_dimension=0, tiled=True).astype(
        jnp.bfloat16
    )
    cot_whole = lax.all_gather(cotangent, "chip", axis=0, tiled=True)
    back_part = jnp.einsum("tv,krv->tkr", cot_whole, fetched_b, preferred_element_type=jnp.float32)
    backward_selected = jnp.einsum(
        "tkr,tk->tr", back_part, onehot_f, precision=lax.Precision.HIGHEST
    )
    backward_half_width = (adapter_scale * backward_selected).astype(jnp.bfloat16)
    back_rank = lax.all_gather(backward_half_width, "chip", axis=1, tiled=True)
    spread_back = onehot_b[:, :, None] * back_rank[:, None, :]
    grad_down = jnp.einsum("td,tkr->kdr", tokens, spread_back, preferred_element_type=jnp.float32)
    up_gradient = adapter_scale * jnp.einsum(
        "tk,tv->kv", spread_rows, cot_whole, preferred_element_type=jnp.float32
    )
    up_gradient = up_gradient.reshape(most, rank_part, width_out)
    route = (my_valid[:, None] & (my_owner[:, None] == owner_ids[None, :])).astype(jnp.float32)
    send_down = jnp.einsum("ko,kdr->odr", route, grad_down, precision=lax.Precision.HIGHEST)
    send_up = jnp.einsum("ko,krv->orv", route, up_gradient, precision=lax.Precision.HIGHEST)
    recv_down, recv_up = (
        lax.all_to_all(
            send_down.astype(jnp.bfloat16), "node", split_axis=0, concat_axis=0, tiled=True
        ).astype(send_down.dtype),
        lax.all_to_all(
            send_up.astype(jnp.bfloat16), "node", split_axis=0, concat_axis=0, tiled=True
        ).astype(send_up.dtype),
    )
    total_down = jnp.einsum("pj,pdr->jdr", picks, recv_down, precision=lax.Precision.HIGHEST)
    total_up = jnp.einsum("pj,prv->jrv", picks, recv_up, precision=lax.Precision.HIGHEST)
    new_a, moment_a, square_a = adam_update(adapter_a, first_a, second_a, total_down)
    new_b, moment_b, square_b = adam_update(adapter_b, first_b, second_b, total_up)
    return (output, new_a, new_b, moment_a, moment_b, square_a, square_b)


MESH = pl.DeviceIdType.MESH
NT = (((1,), (1,)), ((), ()))
TN = (((0,), (0,)), ((), ()))
F32 = jnp.float32
BF16 = jnp.bfloat16


def rows_of(index, size):
    return pl.ds(pl.multiple_of(index * size, size), size)


def step_kernel(
    nodes,
    chips,
    groups,
    slot_ref,
    list_ref,
    count_ref,
    token_slot_ref,
    tokens_in,
    cot_ref,
    w_ref,
    a_in,
    b_in,
    out_ref,
    total_a_ref,
    total_b_ref,
    tokens_ref,
    a_ref,
    b_ref,
    info,
    cot_all,
    w_all,
    send_a,
    recv_a,
    send_b,
    recv_b,
    back_all,
    grad_a,
    got_a,
    grad_b,
    got_b,
    low_all,
    low_send,
    low_recv,
    lora,
    part_send,
    part_recv,
    info_sem,
    cot_sem,
    a_sem,
    b_sem,
    back_sem,
    low_sem,
    ga_sem,
    gb_sem,
    w_sem,
    wg_send_sem,
    wg_recv_sem,
    part_send_sem,
    part_recv_sem,
    local_sem,
):
    me = lax.axis_index("node")
    chip = lax.axis_index("chip")
    group = lax.axis_index("groups")
    owned, rank, depth = a_ref.shape
    rank_part = b_ref.shape[1]
    most = list_ref.shape[1]
    tokens_n = tokens_ref.shape[0]
    out_rows, width = cot_ref.shape
    w_cols = w_ref.shape[1]
    half = depth // groups

    loads = [
        pltpu.make_async_copy(src, dst, local_sem.at[i])
        for i, (src, dst) in enumerate(
            (
                (b_in, b_ref),
                (a_in, a_ref),
                (cot_ref, cot_all.at[rows_of(chip, out_rows)]),
                (tokens_in, tokens_ref),
                (w_ref, w_all.at[me]),
            )
        )
    ]
    for load in loads:
        load.start()
    barrier = pltpu.get_barrier_semaphore()
    for axis, size, here in (("node", nodes, me), ("chip", chips, chip), ("groups", groups, group)):
        for o in range(1, size):
            pl.semaphore_signal(
                barrier, inc=1, device_id={axis: lax.rem(here + o, size)}, device_id_type=MESH
            )

    lane = lax.broadcasted_iota(jnp.int32, (8, 128), 1)
    mine = jnp.full((8, 128), -1, jnp.int32)
    slots = token_slot_ref[...]
    tok_row = jnp.full(slots.shape, -1, jnp.int32)
    for k in range(most):
        row = jnp.where(k < count_ref[0], slot_ref[list_ref[0, k]], -1)
        mine = jnp.where(lane == k, row, mine)
        tok_row = jnp.where(slots == k, row, tok_row)
    info[me] = mine
    masks = [
        jnp.where((tok_row >= p * owned) & (tok_row < (p + 1) * owned), 1.0, 0.0).astype(F32)
        for p in range(nodes)
    ]
    pl.semaphore_wait(barrier, nodes + chips + groups - 3)

    def exchange(axis, size, here, sem, src_of, dst):
        copies = []
        for o in range(1, size):
            peer = lax.rem(here + o, size)
            copies.append(
                pltpu.make_async_remote_copy(
                    src_ref=src_of(peer),
                    dst_ref=dst,
                    send_sem=sem.at[0, o - 1],
                    recv_sem=sem.at[1, o - 1],
                    device_id={axis: peer},
                    device_id_type=MESH,
                )
            )
        return copies

    def start(copies):
        for c in copies:
            c.start()

    def landed(copies):
        for c in copies:
            c.wait_recv()

    info_copies = exchange("node", nodes, me, info_sem, lambda q: info.at[me], info.at[me])
    start(info_copies)
    cot_copies = exchange(
        "chip", chips, chip, cot_sem, lambda q: cot_ref, cot_all.at[rows_of(chip, out_rows)]
    )
    start(cot_copies)

    my_half = rows_of(group, half)

    def w_hop(way, j):
        shard = me - j if way == 0 else me + j
        have = (shard >= 0) if way == 0 else (shard < nodes)
        may = (me < nodes - 1) if way == 0 else (me > 0)
        peer = me + 1 if way == 0 else me - 1
        src = w_ref.at[my_half] if j == 0 else w_all.at[shard, my_half]
        copy = pltpu.make_async_remote_copy(
            src_ref=src,
            dst_ref=w_all.at[shard, my_half],
            send_sem=w_sem.at[0, way, j],
            recv_sem=w_sem.at[1, way, j],
            device_id={"node": peer},
            device_id_type=MESH,
        )
        return have & may, copy

    def w_from(way, j):
        shard = me - 1 - j if way == 0 else me + 1 + j
        have = (shard >= 0) if way == 0 else (shard < nodes)
        return have, shard

    def w_share(way, j, shard):
        copies = []
        for o in range(1, groups):
            copies.append(
                pltpu.make_async_remote_copy(
                    src_ref=w_all.at[shard, my_half],
                    dst_ref=w_all.at[shard, my_half],
                    send_sem=wg_send_sem.at[way, j, o - 1],
                    recv_sem=wg_recv_sem.at[way, j, o - 1],
                    device_id={"groups": lax.rem(group + o, groups)},
                    device_id_type=MESH,
                )
            )
        return copies

    def w_send(way, j):
        go, copy = w_hop(way, j)

        @pl.when(go)
        def _():
            copy.start()

    def w_step(j):
        for way in (0, 1):
            have, shard = w_from(way, j)

            @pl.when(have)
            def _():
                pltpu.make_async_remote_copy(
                    src_ref=w_all.at[shard, my_half],
                    dst_ref=w_all.at[shard, my_half],
                    send_sem=w_sem.at[0, way, j],
                    recv_sem=w_sem.at[1, way, j],
                    device_id={"node": me - 1 if way == 0 else me + 1},
                    device_id_type=MESH,
                ).wait_recv()
                start(w_share(way, j, shard))

            if j + 1 < nodes - 1:
                w_send(way, j + 1)

    w_send(0, 0)
    w_send(1, 0)

    loads[0].wait()
    loads[1].wait()
    landed(info_copies)

    def picks(q):
        found = info[q]
        return [
            jnp.max(jnp.where(found == me * owned + j, 1.0, 0.0).astype(F32)) for j in range(owned)
        ]

    b_copies = exchange(
        "node",
        nodes,
        me,
        b_sem,
        lambda q: send_b.at[rows_of(q, rank_part)],
        recv_b.at[rows_of(me, rank_part)],
    )
    a_copies = exchange(
        "node", nodes, me, a_sem, lambda q: send_a.at[rows_of(q, rank)], recv_a.at[rows_of(me, rank)]
    )
    for o in range(1, nodes + 1):
        q = lax.rem(me + o, nodes)
        pick = picks(q)
        chosen = sum(pick[j] * b_ref[j].astype(F32) for j in range(owned)).astype(BF16)
        if o < nodes:
            send_b[rows_of(q, rank_part), :] = chosen
            b_copies[o - 1].start()
        else:
            recv_b[rows_of(me, rank_part), :] = chosen
    for o in range(1, nodes + 1):
        q = lax.rem(me + o, nodes)
        pick = picks(q)
        chosen = sum(pick[j] * a_ref[j].astype(F32) for j in range(owned)).astype(BF16)
        if o < nodes:
            send_a[rows_of(q, rank), :] = chosen
            a_copies[o - 1].start()
        else:
            recv_a[rows_of(me, rank), :] = chosen

    loads[2].wait()
    landed(cot_copies)
    landed(b_copies)
    every = lax.dot_general(recv_b[...], cot_all[...], NT, preferred_element_type=F32)
    back = sum(
        masks[p] * every[p * rank_part : (p + 1) * rank_part] for p in range(nodes)
    )
    back_all[rows_of(chip, rank_part), :] = (adapter_scale * back).astype(BF16)
    back_copies = exchange(
        "chip",
        chips,
        chip,
        back_sem,
        lambda q: back_all.at[rows_of(chip, rank_part)],
        back_all.at[rows_of(chip, rank_part)],
    )
    start(back_copies)
    w_step(0)
    landed(back_copies)

    whole_back = back_all[...].astype(F32)
    spread_back = jnp.concatenate([masks[p] * whole_back for p in range(nodes)], axis=0).astype(BF16)
    loads[3].wait()
    tile = min(512, depth)
    for t in range(depth // tile):
        cols = slice(t * tile, (t + 1) * tile)
        grad_a[:, cols] = jnp.dot(
            spread_back, tokens_ref[:, cols], preferred_element_type=F32
        ).astype(BF16)
    ga_copies = exchange(
        "node", nodes, me, ga_sem, lambda q: grad_a.at[rows_of(q, rank)], got_a.at[rows_of(me, rank)]
    )
    got_a[rows_of(me, rank), :] = grad_a[rows_of(me, rank), :]
    if nodes > 2:
        w_step(1)
    start(ga_copies)

    landed(a_copies)
    low_all[...] = lax.dot_general(
        recv_a[...], tokens_ref[...], NT, preferred_element_type=F32
    )
    low_send[...] = sum(masks[p] * low_all[p * rank : (p + 1) * rank, :] for p in range(nodes))
    low_copies = exchange(
        "chip",
        chips,
        chip,
        low_sem,
        lambda q: low_send.at[rows_of(q, rank_part)],
        low_recv.at[chip],
    )
    start(low_copies)
    low_recv[chip] = low_send[rows_of(chip, rank_part), :]
    landed(low_copies)
    low_mine = sum(low_recv[c] for c in range(chips)).astype(BF16).astype(F32)
    spread_low = jnp.concatenate([masks[p] * low_mine for p in range(nodes)], axis=0).astype(BF16)
    grad_b[...] = (
        adapter_scale * jnp.dot(spread_low, cot_all[...], preferred_element_type=F32)
    ).astype(BF16)
    gb_copies = exchange(
        "node",
        nodes,
        me,
        gb_sem,
        lambda q: grad_b.at[rows_of(q, rank_part)],
        got_b.at[rows_of(me, rank_part)],
    )
    start(gb_copies)
    got_b[rows_of(me, rank_part), :] = grad_b[rows_of(me, rank_part), :]
    lora[...] = adapter_scale * lax.dot_general(
        spread_low, recv_b[...], TN, preferred_element_type=F32
    )

    def part_copies(shard):
        copies = []
        cols = rows_of(shard, w_cols)
        for o in range(1, chips):
            peer = lax.rem(chip + o, chips)
            copies.append(
                pltpu.make_async_remote_copy(
                    src_ref=part_send.at[rows_of(peer, out_rows), cols],
                    dst_ref=part_recv.at[chip, :, cols],
                    send_sem=part_send_sem.at[shard, o - 1],
                    recv_sem=part_recv_sem.at[shard, o - 1],
                    device_id={"chip": peer},
                    device_id_type=MESH,
                )
            )
        return copies

    def chunk(shard, weight):
        cols = rows_of(shard, w_cols)

        def body(c, carry):
            rows = rows_of(c, out_rows)
            part_send[rows, cols] = (
                jnp.dot(tokens_ref[rows, :], weight[...], preferred_element_type=F32)
                + lora[rows, cols]
            ).astype(BF16)
            return carry

        lax.fori_loop(0, chips, body, 0)
        start(part_copies(shard))

    loads[4].wait()
    chunk(me, w_all.at[me])
    for j in range(nodes - 1):
        if j >= 2:
            w_step(j)
        for way in (0, 1):
            have, shard = w_from(way, j)

            @pl.when(have)
            def _():
                for o in range(1, groups):
                    theirs = rows_of(lax.rem(group + groups - o, groups), half)
                    pltpu.make_async_remote_copy(
                        src_ref=w_all.at[shard, theirs],
                        dst_ref=w_all.at[shard, theirs],
                        send_sem=wg_send_sem.at[way, j, o - 1],
                        recv_sem=wg_recv_sem.at[way, j, o - 1],
                        device_id={"groups": lax.rem(group + o, groups)},
                        device_id_type=MESH,
                    ).wait_recv()
                chunk(shard, w_all.at[shard])

    landed(ga_copies)
    landed(gb_copies)
    weights = [picks(q) for q in range(nodes)]
    for j in range(owned):
        total_a_ref[j] = sum(
            weights[q][j] * got_a[q * rank : (q + 1) * rank, :].astype(F32) for q in range(nodes)
        )
        total_b_ref[j] = sum(
            weights[q][j] * got_b[q * rank_part : (q + 1) * rank_part, :].astype(F32)
            for q in range(nodes)
        )

    for shard in range(nodes):
        landed(part_copies(shard))
    part_recv[chip] = part_send[rows_of(chip, out_rows), :]
    out_ref[...] = sum(part_recv[c].astype(F32) for c in range(chips)).astype(BF16)

    for copies in (
        info_copies,
        cot_copies,
        b_copies,
        a_copies,
        back_copies,
        ga_copies,
        low_copies,
        gb_copies,
    ):
        for c in copies:
            c.wait_send()
    for shard in range(nodes):
        for c in part_copies(shard):
            c.wait_send()
    for j in range(nodes - 1):
        for way in (0, 1):
            go, copy = w_hop(way, j)

            @pl.when(go)
            def _():
                copy.wait_send()

            have, shard = w_from(way, j)

            @pl.when(have)
            def _():
                for c in w_share(way, j, shard):
                    c.wait_send()


def local_fused(
    nodes,
    chips,
    groups,
    tokens,
    cotangent,
    frozen_value_weight,
    adapter_a,
    adapter_b,
    first_a,
    first_b,
    second_a,
    second_b,
    token_slot,
    adapter_slot,
    request_list,
    request_count,
):
    owned, depth, rank = adapter_a.shape
    rank_part = adapter_b.shape[1]
    rows = tokens.shape[0]
    out_rows, width = cotangent.shape
    w_cols = frozen_value_weight.shape[1]
    vmem = pl.BlockSpec(memory_space=pltpu.VMEM)
    smem = pl.BlockSpec(memory_space=pltpu.SMEM)
    dma = pltpu.SemaphoreType.DMA
    output, total_a, total_b = pl.pallas_call(
        functools.partial(step_kernel, nodes, chips, groups),
        out_shape=(
            jax.ShapeDtypeStruct((out_rows, width), BF16),
            jax.ShapeDtypeStruct((owned, rank, depth), F32),
            jax.ShapeDtypeStruct((owned, rank_part, width), F32),
        ),
        in_specs=[smem] * 3 + [vmem] + [pl.BlockSpec(memory_space=pl.ANY)] * 5,
        out_specs=(vmem, vmem, vmem),
        scratch_shapes=[
            pltpu.VMEM((rows, depth), BF16),
            pltpu.VMEM((owned, rank, depth), BF16),
            pltpu.VMEM((owned, rank_part, width), BF16),
            pltpu.VMEM((nodes, 8, 128), jnp.int32),
            pltpu.VMEM((rows, width), BF16),
            pltpu.VMEM((nodes, depth, w_cols), BF16),
            pltpu.VMEM((nodes * rank, depth), BF16),
            pltpu.VMEM((nodes * rank, depth), BF16),
            pltpu.VMEM((nodes * rank_part, width), BF16),
            pltpu.VMEM((nodes * rank_part, width), BF16),
            pltpu.VMEM((rank, rows), BF16),
            pltpu.VMEM((nodes * rank, depth), BF16),
            pltpu.VMEM((nodes * rank, depth), BF16),
            pltpu.VMEM((nodes * rank_part, width), BF16),
            pltpu.VMEM((nodes * rank_part, width), BF16),
            pltpu.VMEM((nodes * rank, rows), F32),
            pltpu.VMEM((rank, rows), F32),
            pltpu.VMEM((chips, rank_part, rows), F32),
            pltpu.VMEM((rows, width), F32),
            pltpu.VMEM((rows, width), BF16),
            pltpu.VMEM((chips, out_rows, width), BF16),
            dma((2, nodes - 1)),
            dma((2, chips - 1)),
            dma((2, nodes - 1)),
            dma((2, nodes - 1)),
            dma((2, chips - 1)),
            dma((2, chips - 1)),
            dma((2, nodes - 1)),
            dma((2, nodes - 1)),
            dma((2, 2, nodes - 1)),
            dma((2, nodes - 1, groups - 1)),
            dma((2, nodes - 1, groups - 1)),
            dma((nodes, chips - 1)),
            dma((nodes, chips - 1)),
            dma((5,)),
        ],
        compiler_params=pltpu.CompilerParams(
            collective_id=0, has_side_effects=True, vmem_limit_bytes=60 * 1024 * 1024
        ),
        cost_estimate=pl.CostEstimate(
            flops=2 * rows * depth * (width + 2 * nodes * rank),
            bytes_accessed=8 * 1024 * 1024,
            transcendentals=0,
        ),
    )(
        adapter_slot,
        request_list,
        request_count,
        token_slot.reshape(1, rows),
        tokens,
        cotangent,
        frozen_value_weight,
        jnp.swapaxes(adapter_a, 1, 2),
        adapter_b,
    )
    new_a, moment_a, square_a = adam_update(
        adapter_a, first_a, second_a, jnp.swapaxes(total_a, 1, 2)
    )
    new_b, moment_b, square_b = adam_update(adapter_b, first_b, second_b, total_b)
    return (output, new_a, new_b, moment_a, moment_b, square_a, square_b)


def solution(mesh):
    nodes, chips, groups = (mesh.shape[name] for name in ("node", "chip", "groups"))
    fits = 2 <= nodes <= 4 and chips >= 2 and groups >= 2
    local = functools.partial(local_fused, nodes, chips, groups) if fits else local_plain
    return jax.shard_map(
        local,
        mesh=mesh,
        in_specs=(
            P(("groups", "node"), "chip"),
            P(("groups", "node", "chip"), None),
            P("chip", "node"),
            P(("groups", "node"), "chip", None),
            P(("groups", "node"), "chip", None),
            P(("groups", "node"), "chip", None),
            P(("groups", "node"), "chip", None),
            P(("groups", "node"), "chip", None),
            P(("groups", "node"), "chip", None),
            P(("groups", "node")),
            P("groups"),
            P(("groups", "node"), None),
            P(("groups", "node")),
        ),
        out_specs=(
            P(("groups", "node", "chip"), None),
            P(("groups", "node"), "chip", None),
            P(("groups", "node"), "chip", None),
            P(("groups", "node"), "chip", None),
            P(("groups", "node"), "chip", None),
            P(("groups", "node"), "chip", None),
            P(("groups", "node"), "chip", None),
        ),
        check_vma=False,
    )
```

```python
import functools

import jax
import jax.numpy as jnp
from jax import lax
from jax.experimental import pallas as pl
from jax.experimental.pallas import tpu as pltpu
from jax.sharding import PartitionSpec as P

adapter_scale = 2.0
beta_one = 0.9
beta_two = 0.999
rate = 0.001
eps_adam = 1e-08
bias_one = 1.0
bias_two = 0.632304575229036


def adam_update(param, first, second, grad):
    first_new = beta_one * first + (1.0 - beta_one) * grad
    second_new = beta_two * second + (1.0 - beta_two) * grad * grad
    update = first_new / bias_one / (jnp.sqrt(second_new / bias_two) + eps_adam)
    return ((param.astype(jnp.float32) - rate * update).astype(jnp.bfloat16), first_new, second_new)


def local_plain(
    tokens,
    cotangent,
    frozen_value_weight,
    adapter_a,
    adapter_b,
    first_a,
    first_b,
    second_a,
    second_b,
    token_slot,
    adapter_slot,
    request_list,
    request_count,
):
    nodes = lax.axis_size("node")
    this_node = lax.axis_index("node")
    this_chip = lax.axis_index("chip")
    owned = adapter_a.shape[0]
    most = request_list.shape[1]
    rank_part = adapter_b.shape[1]
    width_out = adapter_b.shape[2]
    rows_here = tokens.shape[0]
    positions = jnp.arange(most, dtype=jnp.int32)
    owner_ids = jnp.arange(nodes, dtype=jnp.int32)
    local_ids = jnp.arange(owned, dtype=jnp.int32)
    my_rows = jnp.take(adapter_slot, request_list[0], axis=0)
    my_owner = my_rows // owned
    my_valid = positions < request_count[0]
    all_lists, all_counts = (
        lax.all_gather(request_list, "node", axis=0, tiled=True),
        lax.all_gather(request_count, "node", axis=0, tiled=True),
    )
    all_rows = jnp.take(adapter_slot, all_lists, axis=0)
    hits = (positions[None, :] < all_counts[:, None]) & (all_rows // owned == this_node)
    picks = jnp.sum(
        (hits[:, :, None] & ((all_rows % owned)[:, :, None] == local_ids[None, None, :])).astype(
            jnp.float32
        ),
        axis=1,
    )
    picks_low = picks.astype(jnp.bfloat16)
    send_a = jnp.einsum(
        "pj,jdr->pdr", picks_low, adapter_a, preferred_element_type=jnp.float32
    ).astype(jnp.bfloat16)
    send_b = jnp.einsum(
        "pj,jrv->prv", picks_low, adapter_b, preferred_element_type=jnp.float32
    ).astype(jnp.bfloat16)
    recv_a, recv_b = (
        lax.all_to_all(send_a, "node", split_axis=0, concat_axis=0, tiled=True),
        lax.all_to_all(send_b, "node", split_axis=0, concat_axis=0, tiled=True),
    )
    fetched_a = jnp.take(recv_a, my_owner, axis=0)
    fetched_b = jnp.take(recv_b, my_owner, axis=0)
    onehot = (token_slot[:, None] == positions[None, :]) & my_valid[None, :]
    onehot_f = onehot.astype(jnp.float32)
    onehot_b = onehot.astype(jnp.bfloat16)
    low_part = jnp.einsum("td,kdr->tkr", tokens, fetched_a, preferred_element_type=jnp.float32)
    low_sel = jnp.einsum("tkr,tk->tr", low_part, onehot_f, precision=lax.Precision.HIGHEST)
    low_rank = lax.psum(low_sel, "chip")
    low_bf = low_rank.astype(jnp.bfloat16)
    low_mine = lax.dynamic_slice_in_dim(low_bf, this_chip * rank_part, rank_part, 1)
    spread_rows = (onehot_b[:, :, None] * low_mine[:, None, :]).reshape(rows_here, most * rank_part)
    up_flattened = fetched_b.reshape(most * rank_part, width_out)
    frozen_output = jnp.dot(
        tokens,
        lax.all_gather(frozen_value_weight, "node", axis=1, tiled=True),
        preferred_element_type=jnp.float32,
    )
    partial_terms = frozen_output + adapter_scale * jnp.dot(
        spread_rows, up_flattened, preferred_element_type=jnp.float32
    )
    output = lax.psum_scatter(partial_terms, "chip", scatter_dimension=0, tiled=True).astype(
        jnp.bfloat16
    )
    cot_whole = lax.all_gather(cotangent, "chip", axis=0, tiled=True)
    back_part = jnp.einsum("tv,krv->tkr", cot_whole, fetched_b, preferred_element_type=jnp.float32)
    backward_selected = jnp.einsum(
        "tkr,tk->tr", back_part, onehot_f, precision=lax.Precision.HIGHEST
    )
    backward_half_width = (adapter_scale * backward_selected).astype(jnp.bfloat16)
    back_rank = lax.all_gather(backward_half_width, "chip", axis=1, tiled=True)
    spread_back = onehot_b[:, :, None] * back_rank[:, None, :]
    grad_down = jnp.einsum("td,tkr->kdr", tokens, spread_back, preferred_element_type=jnp.float32)
    up_gradient = adapter_scale * jnp.einsum(
        "tk,tv->kv", spread_rows, cot_whole, preferred_element_type=jnp.float32
    )
    up_gradient = up_gradient.reshape(most, rank_part, width_out)
    route = (my_valid[:, None] & (my_owner[:, None] == owner_ids[None, :])).astype(jnp.float32)
    send_down = jnp.einsum("ko,kdr->odr", route, grad_down, precision=lax.Precision.HIGHEST)
    send_up = jnp.einsum("ko,krv->orv", route, up_gradient, precision=lax.Precision.HIGHEST)
    recv_down, recv_up = (
        lax.all_to_all(
            send_down.astype(jnp.bfloat16), "node", split_axis=0, concat_axis=0, tiled=True
        ).astype(send_down.dtype),
        lax.all_to_all(
            send_up.astype(jnp.bfloat16), "node", split_axis=0, concat_axis=0, tiled=True
        ).astype(send_up.dtype),
    )
    total_down = jnp.einsum("pj,pdr->jdr", picks, recv_down, precision=lax.Precision.HIGHEST)
    total_up = jnp.einsum("pj,prv->jrv", picks, recv_up, precision=lax.Precision.HIGHEST)
    new_a, moment_a, square_a = adam_update(adapter_a, first_a, second_a, total_down)
    new_b, moment_b, square_b = adam_update(adapter_b, first_b, second_b, total_up)
    return (output, new_a, new_b, moment_a, moment_b, square_a, square_b)


MESH = pl.DeviceIdType.MESH
NT = (((1,), (1,)), ((), ()))
TN = (((0,), (0,)), ((), ()))
F32 = jnp.float32
BF16 = jnp.bfloat16


def rows_of(index, size):
    return pl.ds(pl.multiple_of(index * size, size), size)


def step_kernel(
    nodes,
    chips,
    groups,
    slot_ref,
    list_ref,
    count_ref,
    token_slot_ref,
    tokens_in,
    cot_ref,
    w_ref,
    a_in,
    b_in,
    out_ref,
    total_a_ref,
    total_b_ref,
    tokens_ref,
    a_ref,
    b_ref,
    info,
    cot_all,
    w_all,
    send_a,
    recv_a,
    send_b,
    recv_b,
    back_all,
    grad_a,
    got_a,
    grad_b,
    got_b,
    low_all,
    low_send,
    low_recv,
    lora,
    part_send,
    part_recv,
    info_sem,
    cot_sem,
    a_sem,
    b_sem,
    back_sem,
    low_sem,
    ga_sem,
    gb_sem,
    w_sem,
    wg_send_sem,
    wg_recv_sem,
    part_send_sem,
    part_recv_sem,
    local_sem,
):
    me = lax.axis_index("node")
    chip = lax.axis_index("chip")
    group = lax.axis_index("groups")
    owned, rank, depth = a_ref.shape
    rank_part = b_ref.shape[1]
    most = list_ref.shape[1]
    tokens_n = tokens_ref.shape[0]
    out_rows, width = cot_ref.shape
    w_cols = w_ref.shape[1]
    half = depth // groups

    loads = [
        pltpu.make_async_copy(src, dst, local_sem.at[i])
        for i, (src, dst) in enumerate(
            (
                (b_in, b_ref),
                (a_in, a_ref),
                (cot_ref, cot_all.at[rows_of(chip, out_rows)]),
                (tokens_in, tokens_ref),
                (w_ref, w_all.at[me]),
            )
        )
    ]
    for load in loads:
        load.start()
    barrier = pltpu.get_barrier_semaphore()
    for axis, size, here in (("node", nodes, me), ("chip", chips, chip), ("groups", groups, group)):
        for o in range(1, size):
            pl.semaphore_signal(
                barrier, inc=1, device_id={axis: lax.rem(here + o, size)}, device_id_type=MESH
            )

    lane = lax.broadcasted_iota(jnp.int32, (8, 128), 1)
    mine = jnp.full((8, 128), -1, jnp.int32)
    slots = token_slot_ref[...]
    tok_row = jnp.full(slots.shape, -1, jnp.int32)
    for k in range(most):
        row = jnp.where(k < count_ref[0], slot_ref[list_ref[0, k]], -1)
        mine = jnp.where(lane == k, row, mine)
        tok_row = jnp.where(slots == k, row, tok_row)
    info[me] = mine
    masks = [
        jnp.where((tok_row >= p * owned) & (tok_row < (p + 1) * owned), 1.0, 0.0).astype(F32)
        for p in range(nodes)
    ]
    pl.semaphore_wait(barrier, nodes + chips + groups - 3)

    def exchange(axis, size, here, sem, src_of, dst):
        copies = []
        for o in range(1, size):
            peer = lax.rem(here + o, size)
            copies.append(
                pltpu.make_async_remote_copy(
                    src_ref=src_of(peer),
                    dst_ref=dst,
                    send_sem=sem.at[0, o - 1],
                    recv_sem=sem.at[1, o - 1],
                    device_id={axis: peer},
                    device_id_type=MESH,
                )
            )
        return copies

    def start(copies):
        for c in copies:
            c.start()

    def landed(copies):
        for c in copies:
            c.wait_recv()

    info_copies = exchange("node", nodes, me, info_sem, lambda q: info.at[me], info.at[me])
    start(info_copies)
    cot_copies = exchange(
        "chip", chips, chip, cot_sem, lambda q: cot_ref, cot_all.at[rows_of(chip, out_rows)]
    )
    start(cot_copies)

    my_half = rows_of(group, half)

    def w_hop(way, j):
        shard = me - j if way == 0 else me + j
        have = (shard >= 0) if way == 0 else (shard < nodes)
        may = (me < nodes - 1) if way == 0 else (me > 0)
        peer = me + 1 if way == 0 else me - 1
        src = w_ref.at[my_half] if j == 0 else w_all.at[shard, my_half]
        copy = pltpu.make_async_remote_copy(
            src_ref=src,
            dst_ref=w_all.at[shard, my_half],
            send_sem=w_sem.at[0, way, j],
            recv_sem=w_sem.at[1, way, j],
            device_id={"node": peer},
            device_id_type=MESH,
        )
        return have & may, copy

    def w_from(way, j):
        shard = me - 1 - j if way == 0 else me + 1 + j
        have = (shard >= 0) if way == 0 else (shard < nodes)
        return have, shard

    def w_share(way, j, shard):
        copies = []
        for o in range(1, groups):
            copies.append(
                pltpu.make_async_remote_copy(
                    src_ref=w_all.at[shard, my_half],
                    dst_ref=w_all.at[shard, my_half],
                    send_sem=wg_send_sem.at[way, j, o - 1],
                    recv_sem=wg_recv_sem.at[way, j, o - 1],
                    device_id={"groups": lax.rem(group + o, groups)},
                    device_id_type=MESH,
                )
            )
        return copies

    def w_send(way, j):
        go, copy = w_hop(way, j)

        @pl.when(go)
        def _():
            copy.start()

    def w_step(j):
        for way in (0, 1):
            have, shard = w_from(way, j)

            @pl.when(have)
            def _():
                pltpu.make_async_remote_copy(
                    src_ref=w_all.at[shard, my_half],
                    dst_ref=w_all.at[shard, my_half],
                    send_sem=w_sem.at[0, way, j],
                    recv_sem=w_sem.at[1, way, j],
                    device_id={"node": me - 1 if way == 0 else me + 1},
                    device_id_type=MESH,
                ).wait_recv()
                start(w_share(way, j, shard))

            if j + 1 < nodes - 1:
                w_send(way, j + 1)

    w_send(0, 0)
    w_send(1, 0)

    loads[0].wait()
    loads[1].wait()
    landed(info_copies)

    def picks(q):
        found = info[q]
        return [
            jnp.max(jnp.where(found == me * owned + j, 1.0, 0.0).astype(F32)) for j in range(owned)
        ]

    b_copies = exchange(
        "node",
        nodes,
        me,
        b_sem,
        lambda q: send_b.at[rows_of(q, rank_part)],
        recv_b.at[rows_of(me, rank_part)],
    )
    a_copies = exchange(
        "node", nodes, me, a_sem, lambda q: send_a.at[rows_of(q, rank)], recv_a.at[rows_of(me, rank)]
    )
    for o in range(1, nodes + 1):
        q = lax.rem(me + o, nodes)
        pick = picks(q)
        chosen = sum(pick[j] * b_ref[j].astype(F32) for j in range(owned)).astype(BF16)
        if o < nodes:
            send_b[rows_of(q, rank_part), :] = chosen
            b_copies[o - 1].start()
        else:
            recv_b[rows_of(me, rank_part), :] = chosen
    for o in range(1, nodes + 1):
        q = lax.rem(me + o, nodes)
        pick = picks(q)
        chosen = sum(pick[j] * a_ref[j].astype(F32) for j in range(owned)).astype(BF16)
        if o < nodes:
            send_a[rows_of(q, rank), :] = chosen
            a_copies[o - 1].start()
        else:
            recv_a[rows_of(me, rank), :] = chosen

    loads[2].wait()
    landed(cot_copies)
    landed(b_copies)
    every = lax.dot_general(recv_b[...], cot_all[...], NT, preferred_element_type=F32)
    back = sum(
        masks[p] * every[p * rank_part : (p + 1) * rank_part] for p in range(nodes)
    )
    back_all[rows_of(chip, rank_part), :] = (adapter_scale * back).astype(BF16)
    back_copies = exchange(
        "chip",
        chips,
        chip,
        back_sem,
        lambda q: back_all.at[rows_of(chip, rank_part)],
        back_all.at[rows_of(chip, rank_part)],
    )
    start(back_copies)
    w_step(0)
    landed(back_copies)

    whole_back = back_all[...].astype(F32)
    spread_back = jnp.concatenate([masks[p] * whole_back for p in range(nodes)], axis=0).astype(BF16)
    loads[3].wait()
    tile = min(512, depth)
    for t in range(depth // tile):
        cols = slice(t * tile, (t + 1) * tile)
        grad_a[:, cols] = jnp.dot(
            spread_back, tokens_ref[:, cols], preferred_element_type=F32
        ).astype(BF16)
    ga_copies = exchange(
        "node", nodes, me, ga_sem, lambda q: grad_a.at[rows_of(q, rank)], got_a.at[rows_of(me, rank)]
    )
    got_a[rows_of(me, rank), :] = grad_a[rows_of(me, rank), :]
    if nodes > 2:
        w_step(1)

    landed(a_copies)
    low_all[...] = lax.dot_general(
        recv_a[...], tokens_ref[...], NT, preferred_element_type=F32
    )
    low_send[...] = sum(masks[p] * low_all[p * rank : (p + 1) * rank, :] for p in range(nodes))
    low_copies = exchange(
        "chip",
        chips,
        chip,
        low_sem,
        lambda q: low_send.at[rows_of(q, rank_part)],
        low_recv.at[chip],
    )
    start(low_copies)
    low_recv[chip] = low_send[rows_of(chip, rank_part), :]
    landed(low_copies)
    low_mine = sum(low_recv[c] for c in range(chips)).astype(BF16).astype(F32)
    spread_low = jnp.concatenate([masks[p] * low_mine for p in range(nodes)], axis=0).astype(BF16)
    grad_b[...] = (
        adapter_scale * jnp.dot(spread_low, cot_all[...], preferred_element_type=F32)
    ).astype(BF16)
    gb_copies = exchange(
        "node",
        nodes,
        me,
        gb_sem,
        lambda q: grad_b.at[rows_of(q, rank_part)],
        got_b.at[rows_of(me, rank_part)],
    )
    start(gb_copies)
    got_b[rows_of(me, rank_part), :] = grad_b[rows_of(me, rank_part), :]
    lora[...] = adapter_scale * lax.dot_general(
        spread_low, recv_b[...], TN, preferred_element_type=F32
    )

    def part_copies(shard):
        copies = []
        cols = rows_of(shard, w_cols)
        for o in range(1, chips):
            peer = lax.rem(chip + o, chips)
            copies.append(
                pltpu.make_async_remote_copy(
                    src_ref=part_send.at[rows_of(peer, out_rows), cols],
                    dst_ref=part_recv.at[chip, :, cols],
                    send_sem=part_send_sem.at[shard, o - 1],
                    recv_sem=part_recv_sem.at[shard, o - 1],
                    device_id={"chip": peer},
                    device_id_type=MESH,
                )
            )
        return copies

    def chunk(shard, weight):
        cols = rows_of(shard, w_cols)

        def body(c, carry):
            rows = rows_of(c, out_rows)
            part_send[rows, cols] = (
                jnp.dot(tokens_ref[rows, :], weight[...], preferred_element_type=F32)
                + lora[rows, cols]
            ).astype(BF16)
            return carry

        lax.fori_loop(0, chips, body, 0)
        start(part_copies(shard))

    loads[4].wait()
    chunk(me, w_all.at[me])
    for j in range(nodes - 1):
        if j >= 2:
            w_step(j)
        if j == nodes - 2:
            start(ga_copies)
        for way in (0, 1):
            have, shard = w_from(way, j)

            @pl.when(have)
            def _():
                for o in range(1, groups):
                    theirs = rows_of(lax.rem(group + groups - o, groups), half)
                    pltpu.make_async_remote_copy(
                        src_ref=w_all.at[shard, theirs],
                        dst_ref=w_all.at[shard, theirs],
                        send_sem=wg_send_sem.at[way, j, o - 1],
                        recv_sem=wg_recv_sem.at[way, j, o - 1],
                        device_id={"groups": lax.rem(group + o, groups)},
                        device_id_type=MESH,
                    ).wait_recv()
                chunk(shard, w_all.at[shard])

    landed(ga_copies)
    landed(gb_copies)
    weights = [picks(q) for q in range(nodes)]
    for j in range(owned):
        total_a_ref[j] = sum(
            weights[q][j] * got_a[q * rank : (q + 1) * rank, :].astype(F32) for q in range(nodes)
        )
        total_b_ref[j] = sum(
            weights[q][j] * got_b[q * rank_part : (q + 1) * rank_part, :].astype(F32)
            for q in range(nodes)
        )

    for shard in range(nodes):
        landed(part_copies(shard))
    part_recv[chip] = part_send[rows_of(chip, out_rows), :]
    out_ref[...] = sum(part_recv[c].astype(F32) for c in range(chips)).astype(BF16)

    for copies in (
        info_copies,
        cot_copies,
        b_copies,
        a_copies,
        back_copies,
        ga_copies,
        low_copies,
        gb_copies,
    ):
        for c in copies:
            c.wait_send()
    for shard in range(nodes):
        for c in part_copies(shard):
            c.wait_send()
    for j in range(nodes - 1):
        for way in (0, 1):
            go, copy = w_hop(way, j)

            @pl.when(go)
            def _():
                copy.wait_send()

            have, shard = w_from(way, j)

            @pl.when(have)
            def _():
                for c in w_share(way, j, shard):
                    c.wait_send()


def local_fused(
    nodes,
    chips,
    groups,
    tokens,
    cotangent,
    frozen_value_weight,
    adapter_a,
    adapter_b,
    first_a,
    first_b,
    second_a,
    second_b,
    token_slot,
    adapter_slot,
    request_list,
    request_count,
):
    owned, depth, rank = adapter_a.shape
    rank_part = adapter_b.shape[1]
    rows = tokens.shape[0]
    out_rows, width = cotangent.shape
    w_cols = frozen_value_weight.shape[1]
    vmem = pl.BlockSpec(memory_space=pltpu.VMEM)
    smem = pl.BlockSpec(memory_space=pltpu.SMEM)
    dma = pltpu.SemaphoreType.DMA
    output, total_a, total_b = pl.pallas_call(
        functools.partial(step_kernel, nodes, chips, groups),
        out_shape=(
            jax.ShapeDtypeStruct((out_rows, width), BF16),
            jax.ShapeDtypeStruct((owned, rank, depth), F32),
            jax.ShapeDtypeStruct((owned, rank_part, width), F32),
        ),
        in_specs=[smem] * 3 + [vmem] + [pl.BlockSpec(memory_space=pl.ANY)] * 5,
        out_specs=(vmem, vmem, vmem),
        scratch_shapes=[
            pltpu.VMEM((rows, depth), BF16),
            pltpu.VMEM((owned, rank, depth), BF16),
            pltpu.VMEM((owned, rank_part, width), BF16),
            pltpu.VMEM((nodes, 8, 128), jnp.int32),
            pltpu.VMEM((rows, width), BF16),
            pltpu.VMEM((nodes, depth, w_cols), BF16),
            pltpu.VMEM((nodes * rank, depth), BF16),
            pltpu.VMEM((nodes * rank, depth), BF16),
            pltpu.VMEM((nodes * rank_part, width), BF16),
            pltpu.VMEM((nodes * rank_part, width), BF16),
            pltpu.VMEM((rank, rows), BF16),
            pltpu.VMEM((nodes * rank, depth), BF16),
            pltpu.VMEM((nodes * rank, depth), BF16),
            pltpu.VMEM((nodes * rank_part, width), BF16),
            pltpu.VMEM((nodes * rank_part, width), BF16),
            pltpu.VMEM((nodes * rank, rows), F32),
            pltpu.VMEM((rank, rows), F32),
            pltpu.VMEM((chips, rank_part, rows), F32),
            pltpu.VMEM((rows, width), F32),
            pltpu.VMEM((rows, width), BF16),
            pltpu.VMEM((chips, out_rows, width), BF16),
            dma((2, nodes - 1)),
            dma((2, chips - 1)),
            dma((2, nodes - 1)),
            dma((2, nodes - 1)),
            dma((2, chips - 1)),
            dma((2, chips - 1)),
            dma((2, nodes - 1)),
            dma((2, nodes - 1)),
            dma((2, 2, nodes - 1)),
            dma((2, nodes - 1, groups - 1)),
            dma((2, nodes - 1, groups - 1)),
            dma((nodes, chips - 1)),
            dma((nodes, chips - 1)),
            dma((5,)),
        ],
        compiler_params=pltpu.CompilerParams(
            collective_id=0, has_side_effects=True, vmem_limit_bytes=60 * 1024 * 1024
        ),
        cost_estimate=pl.CostEstimate(
            flops=2 * rows * depth * (width + 2 * nodes * rank),
            bytes_accessed=8 * 1024 * 1024,
            transcendentals=0,
        ),
    )(
        adapter_slot,
        request_list,
        request_count,
        token_slot.reshape(1, rows),
        tokens,
        cotangent,
        frozen_value_weight,
        jnp.swapaxes(adapter_a, 1, 2),
        adapter_b,
    )
    new_a, moment_a, square_a = adam_update(
        adapter_a, first_a, second_a, jnp.swapaxes(total_a, 1, 2)
    )
    new_b, moment_b, square_b = adam_update(adapter_b, first_b, second_b, total_b)
    return (output, new_a, new_b, moment_a, moment_b, square_a, square_b)


def solution(mesh):
    nodes, chips, groups = (mesh.shape[name] for name in ("node", "chip", "groups"))
    fits = 2 <= nodes <= 4 and chips >= 2 and groups >= 2
    local = functools.partial(local_fused, nodes, chips, groups) if fits else local_plain
    return jax.shard_map(
        local,
        mesh=mesh,
        in_specs=(
            P(("groups", "node"), "chip"),
            P(("groups", "node", "chip"), None),
            P("chip", "node"),
            P(("groups", "node"), "chip", None),
            P(("groups", "node"), "chip", None),
            P(("groups", "node"), "chip", None),
            P(("groups", "node"), "chip", None),
            P(("groups", "node"), "chip", None),
            P(("groups", "node"), "chip", None),
            P(("groups", "node")),
            P("groups"),
            P(("groups", "node"), None),
            P(("groups", "node")),
        ),
        out_specs=(
            P(("groups", "node", "chip"), None),
            P(("groups", "node"), "chip", None),
            P(("groups", "node"), "chip", None),
            P(("groups", "node"), "chip", None),
            P(("groups", "node"), "chip", None),
            P(("groups", "node"), "chip", None),
            P(("groups", "node"), "chip", None),
        ),
        check_vma=False,
    )
```

```python
import functools

import jax
import jax.numpy as jnp
from jax import lax
from jax.experimental import pallas as pl
from jax.experimental.pallas import tpu as pltpu
from jax.sharding import PartitionSpec as P

adapter_scale = 2.0
beta_one = 0.9
beta_two = 0.999
rate = 0.001
eps_adam = 1e-08
bias_one = 1.0
bias_two = 0.632304575229036


def adam_update(param, first, second, grad):
    first_new = beta_one * first + (1.0 - beta_one) * grad
    second_new = beta_two * second + (1.0 - beta_two) * grad * grad
    update = first_new / bias_one / (jnp.sqrt(second_new / bias_two) + eps_adam)
    return ((param.astype(jnp.float32) - rate * update).astype(jnp.bfloat16), first_new, second_new)


def local_plain(
    tokens,
    cotangent,
    frozen_value_weight,
    adapter_a,
    adapter_b,
    first_a,
    first_b,
    second_a,
    second_b,
    token_slot,
    adapter_slot,
    request_list,
    request_count,
):
    nodes = lax.axis_size("node")
    this_node = lax.axis_index("node")
    this_chip = lax.axis_index("chip")
    owned = adapter_a.shape[0]
    most = request_list.shape[1]
    rank_part = adapter_b.shape[1]
    width_out = adapter_b.shape[2]
    rows_here = tokens.shape[0]
    positions = jnp.arange(most, dtype=jnp.int32)
    owner_ids = jnp.arange(nodes, dtype=jnp.int32)
    local_ids = jnp.arange(owned, dtype=jnp.int32)
    my_rows = jnp.take(adapter_slot, request_list[0], axis=0)
    my_owner = my_rows // owned
    my_valid = positions < request_count[0]
    all_lists, all_counts = (
        lax.all_gather(request_list, "node", axis=0, tiled=True),
        lax.all_gather(request_count, "node", axis=0, tiled=True),
    )
    all_rows = jnp.take(adapter_slot, all_lists, axis=0)
    hits = (positions[None, :] < all_counts[:, None]) & (all_rows // owned == this_node)
    picks = jnp.sum(
        (hits[:, :, None] & ((all_rows % owned)[:, :, None] == local_ids[None, None, :])).astype(
            jnp.float32
        ),
        axis=1,
    )
    picks_low = picks.astype(jnp.bfloat16)
    send_a = jnp.einsum(
        "pj,jdr->pdr", picks_low, adapter_a, preferred_element_type=jnp.float32
    ).astype(jnp.bfloat16)
    send_b = jnp.einsum(
        "pj,jrv->prv", picks_low, adapter_b, preferred_element_type=jnp.float32
    ).astype(jnp.bfloat16)
    recv_a, recv_b = (
        lax.all_to_all(send_a, "node", split_axis=0, concat_axis=0, tiled=True),
        lax.all_to_all(send_b, "node", split_axis=0, concat_axis=0, tiled=True),
    )
    fetched_a = jnp.take(recv_a, my_owner, axis=0)
    fetched_b = jnp.take(recv_b, my_owner, axis=0)
    onehot = (token_slot[:, None] == positions[None, :]) & my_valid[None, :]
    onehot_f = onehot.astype(jnp.float32)
    onehot_b = onehot.astype(jnp.bfloat16)
    low_part = jnp.einsum("td,kdr->tkr", tokens, fetched_a, preferred_element_type=jnp.float32)
    low_sel = jnp.einsum("tkr,tk->tr", low_part, onehot_f, precision=lax.Precision.HIGHEST)
    low_rank = lax.psum(low_sel, "chip")
    low_bf = low_rank.astype(jnp.bfloat16)
    low_mine = lax.dynamic_slice_in_dim(low_bf, this_chip * rank_part, rank_part, 1)
    spread_rows = (onehot_b[:, :, None] * low_mine[:, None, :]).reshape(rows_here, most * rank_part)
    up_flattened = fetched_b.reshape(most * rank_part, width_out)
    frozen_output = jnp.dot(
        tokens,
        lax.all_gather(frozen_value_weight, "node", axis=1, tiled=True),
        preferred_element_type=jnp.float32,
    )
    partial_terms = frozen_output + adapter_scale * jnp.dot(
        spread_rows, up_flattened, preferred_element_type=jnp.float32
    )
    output = lax.psum_scatter(partial_terms, "chip", scatter_dimension=0, tiled=True).astype(
        jnp.bfloat16
    )
    cot_whole = lax.all_gather(cotangent, "chip", axis=0, tiled=True)
    back_part = jnp.einsum("tv,krv->tkr", cot_whole, fetched_b, preferred_element_type=jnp.float32)
    backward_selected = jnp.einsum(
        "tkr,tk->tr", back_part, onehot_f, precision=lax.Precision.HIGHEST
    )
    backward_half_width = (adapter_scale * backward_selected).astype(jnp.bfloat16)
    back_rank = lax.all_gather(backward_half_width, "chip", axis=1, tiled=True)
    spread_back = onehot_b[:, :, None] * back_rank[:, None, :]
    grad_down = jnp.einsum("td,tkr->kdr", tokens, spread_back, preferred_element_type=jnp.float32)
    up_gradient = adapter_scale * jnp.einsum(
        "tk,tv->kv", spread_rows, cot_whole, preferred_element_type=jnp.float32
    )
    up_gradient = up_gradient.reshape(most, rank_part, width_out)
    route = (my_valid[:, None] & (my_owner[:, None] == owner_ids[None, :])).astype(jnp.float32)
    send_down = jnp.einsum("ko,kdr->odr", route, grad_down, precision=lax.Precision.HIGHEST)
    send_up = jnp.einsum("ko,krv->orv", route, up_gradient, precision=lax.Precision.HIGHEST)
    recv_down, recv_up = (
        lax.all_to_all(
            send_down.astype(jnp.bfloat16), "node", split_axis=0, concat_axis=0, tiled=True
        ).astype(send_down.dtype),
        lax.all_to_all(
            send_up.astype(jnp.bfloat16), "node", split_axis=0, concat_axis=0, tiled=True
        ).astype(send_up.dtype),
    )
    total_down = jnp.einsum("pj,pdr->jdr", picks, recv_down, precision=lax.Precision.HIGHEST)
    total_up = jnp.einsum("pj,prv->jrv", picks, recv_up, precision=lax.Precision.HIGHEST)
    new_a, moment_a, square_a = adam_update(adapter_a, first_a, second_a, total_down)
    new_b, moment_b, square_b = adam_update(adapter_b, first_b, second_b, total_up)
    return (output, new_a, new_b, moment_a, moment_b, square_a, square_b)


MESH = pl.DeviceIdType.MESH
NT = (((1,), (1,)), ((), ()))
TN = (((0,), (0,)), ((), ()))
F32 = jnp.float32
BF16 = jnp.bfloat16


def rows_of(index, size):
    return pl.ds(pl.multiple_of(index * size, size), size)


def step_kernel(
    nodes,
    chips,
    groups,
    slot_ref,
    list_ref,
    count_ref,
    token_slot_ref,
    tokens_in,
    cot_ref,
    w_ref,
    a_in,
    b_in,
    out_ref,
    total_a_ref,
    total_b_ref,
    tokens_ref,
    a_ref,
    b_ref,
    info,
    cot_all,
    w_all,
    send_a,
    recv_a,
    send_b,
    recv_b,
    back_all,
    grad_a,
    got_a,
    grad_b,
    got_b,
    low_all,
    low_send,
    low_recv,
    lora,
    part_send,
    part_recv,
    info_sem,
    cot_sem,
    a_sem,
    b_sem,
    back_sem,
    low_sem,
    ga_sem,
    gb_sem,
    w_sem,
    wg_send_sem,
    wg_recv_sem,
    part_send_sem,
    part_recv_sem,
    local_sem,
):
    me = lax.axis_index("node")
    chip = lax.axis_index("chip")
    group = lax.axis_index("groups")
    owned, rank, depth = a_ref.shape
    rank_part = b_ref.shape[1]
    most = list_ref.shape[1]
    tokens_n = tokens_ref.shape[0]
    out_rows, width = cot_ref.shape
    w_cols = w_ref.shape[1]
    half = depth // groups

    loads = [
        pltpu.make_async_copy(src, dst, local_sem.at[i])
        for i, (src, dst) in enumerate(
            (
                (b_in, b_ref),
                (a_in, a_ref),
                (cot_ref, cot_all.at[rows_of(chip, out_rows)]),
                (tokens_in, tokens_ref),
                (w_ref, w_all.at[me]),
            )
        )
    ]
    for load in loads:
        load.start()
    barrier = pltpu.get_barrier_semaphore()
    for axis, size, here in (("node", nodes, me), ("chip", chips, chip), ("groups", groups, group)):
        for o in range(1, size):
            pl.semaphore_signal(
                barrier, inc=1, device_id={axis: lax.rem(here + o, size)}, device_id_type=MESH
            )

    lane = lax.broadcasted_iota(jnp.int32, (8, 128), 1)
    mine = jnp.full((8, 128), -1, jnp.int32)
    slots = token_slot_ref[...]
    tok_row = jnp.full(slots.shape, -1, jnp.int32)
    for k in range(most):
        row = jnp.where(k < count_ref[0], slot_ref[list_ref[0, k]], -1)
        mine = jnp.where(lane == k, row, mine)
        tok_row = jnp.where(slots == k, row, tok_row)
    info[me] = mine
    masks = [
        jnp.where((tok_row >= p * owned) & (tok_row < (p + 1) * owned), 1.0, 0.0).astype(F32)
        for p in range(nodes)
    ]
    pl.semaphore_wait(barrier, nodes + chips + groups - 3)

    def exchange(axis, size, here, sem, src_of, dst):
        copies = []
        for o in range(1, size):
            peer = lax.rem(here + o, size)
            copies.append(
                pltpu.make_async_remote_copy(
                    src_ref=src_of(peer),
                    dst_ref=dst,
                    send_sem=sem.at[0, o - 1],
                    recv_sem=sem.at[1, o - 1],
                    device_id={axis: peer},
                    device_id_type=MESH,
                )
            )
        return copies

    def start(copies):
        for c in copies:
            c.start()

    def landed(copies):
        for c in copies:
            c.wait_recv()

    info_copies = exchange("node", nodes, me, info_sem, lambda q: info.at[me], info.at[me])
    start(info_copies)
    cot_copies = exchange(
        "chip", chips, chip, cot_sem, lambda q: cot_ref, cot_all.at[rows_of(chip, out_rows)]
    )
    start(cot_copies)

    my_half = rows_of(group, half)

    def w_hop(way, j):
        shard = me - j if way == 0 else me + j
        have = (shard >= 0) if way == 0 else (shard < nodes)
        may = (me < nodes - 1) if way == 0 else (me > 0)
        peer = me + 1 if way == 0 else me - 1
        src = w_ref.at[my_half] if j == 0 else w_all.at[shard, my_half]
        copy = pltpu.make_async_remote_copy(
            src_ref=src,
            dst_ref=w_all.at[shard, my_half],
            send_sem=w_sem.at[0, way, j],
            recv_sem=w_sem.at[1, way, j],
            device_id={"node": peer},
            device_id_type=MESH,
        )
        return have & may, copy

    def w_from(way, j):
        shard = me - 1 - j if way == 0 else me + 1 + j
        have = (shard >= 0) if way == 0 else (shard < nodes)
        return have, shard

    def w_share(way, j, shard):
        copies = []
        for o in range(1, groups):
            copies.append(
                pltpu.make_async_remote_copy(
                    src_ref=w_all.at[shard, my_half],
                    dst_ref=w_all.at[shard, my_half],
                    send_sem=wg_send_sem.at[way, j, o - 1],
                    recv_sem=wg_recv_sem.at[way, j, o - 1],
                    device_id={"groups": lax.rem(group + o, groups)},
                    device_id_type=MESH,
                )
            )
        return copies

    def w_send(way, j):
        go, copy = w_hop(way, j)

        @pl.when(go)
        def _():
            copy.start()

    def w_step(j):
        for way in (0, 1):
            have, shard = w_from(way, j)

            @pl.when(have)
            def _():
                pltpu.make_async_remote_copy(
                    src_ref=w_all.at[shard, my_half],
                    dst_ref=w_all.at[shard, my_half],
                    send_sem=w_sem.at[0, way, j],
                    recv_sem=w_sem.at[1, way, j],
                    device_id={"node": me - 1 if way == 0 else me + 1},
                    device_id_type=MESH,
                ).wait_recv()
                start(w_share(way, j, shard))

            if j + 1 < nodes - 1:
                w_send(way, j + 1)

    w_send(0, 0)
    w_send(1, 0)

    loads[0].wait()
    loads[1].wait()
    landed(info_copies)

    def picks(q):
        found = info[q]
        return [
            jnp.max(jnp.where(found == me * owned + j, 1.0, 0.0).astype(F32)) for j in range(owned)
        ]

    b_copies = exchange(
        "node",
        nodes,
        me,
        b_sem,
        lambda q: send_b.at[rows_of(q, rank_part)],
        recv_b.at[rows_of(me, rank_part)],
    )
    a_copies = exchange(
        "node", nodes, me, a_sem, lambda q: send_a.at[rows_of(q, rank)], recv_a.at[rows_of(me, rank)]
    )
    for o in range(1, nodes + 1):
        q = lax.rem(me + o, nodes)
        pick = picks(q)
        chosen = sum(pick[j] * b_ref[j].astype(F32) for j in range(owned)).astype(BF16)
        if o < nodes:
            send_b[rows_of(q, rank_part), :] = chosen
            b_copies[o - 1].start()
        else:
            recv_b[rows_of(me, rank_part), :] = chosen
    for o in range(1, nodes + 1):
        q = lax.rem(me + o, nodes)
        pick = picks(q)
        chosen = sum(pick[j] * a_ref[j].astype(F32) for j in range(owned)).astype(BF16)
        if o < nodes:
            send_a[rows_of(q, rank), :] = chosen
            a_copies[o - 1].start()
        else:
            recv_a[rows_of(me, rank), :] = chosen

    loads[2].wait()
    landed(cot_copies)
    landed(b_copies)
    every = lax.dot_general(recv_b[...], cot_all[...], NT, preferred_element_type=F32)
    back = sum(
        masks[p] * every[p * rank_part : (p + 1) * rank_part] for p in range(nodes)
    )
    back_all[rows_of(chip, rank_part), :] = (adapter_scale * back).astype(BF16)
    back_copies = exchange(
        "chip",
        chips,
        chip,
        back_sem,
        lambda q: back_all.at[rows_of(chip, rank_part)],
        back_all.at[rows_of(chip, rank_part)],
    )
    start(back_copies)
    w_step(0)
    landed(back_copies)

    whole_back = back_all[...].astype(F32)
    spread_back = jnp.concatenate([masks[p] * whole_back for p in range(nodes)], axis=0).astype(BF16)
    loads[3].wait()
    tile = min(512, depth)
    for t in range(depth // tile):
        cols = slice(t * tile, (t + 1) * tile)
        grad_a[:, cols] = jnp.dot(
            spread_back, tokens_ref[:, cols], preferred_element_type=F32
        ).astype(BF16)
    ga_copies = exchange(
        "node", nodes, me, ga_sem, lambda q: grad_a.at[rows_of(q, rank)], got_a.at[rows_of(me, rank)]
    )
    got_a[rows_of(me, rank), :] = grad_a[rows_of(me, rank), :]
    if nodes > 2:
        w_step(1)

    def start_ga(to_inner):
        for o in range(1, nodes):
            q = lax.rem(me + o, nodes)
            inner = (q > 0) & (q < nodes - 1)

            @pl.when(inner if to_inner else jnp.logical_not(inner))
            def _():
                ga_copies[o - 1].start()

    start_ga(True)
    if nodes <= 3:
        start_ga(False)

    landed(a_copies)
    low_all[...] = lax.dot_general(
        recv_a[...], tokens_ref[...], NT, preferred_element_type=F32
    )
    low_send[...] = sum(masks[p] * low_all[p * rank : (p + 1) * rank, :] for p in range(nodes))
    low_copies = exchange(
        "chip",
        chips,
        chip,
        low_sem,
        lambda q: low_send.at[rows_of(q, rank_part)],
        low_recv.at[chip],
    )
    start(low_copies)
    low_recv[chip] = low_send[rows_of(chip, rank_part), :]
    landed(low_copies)
    low_mine = sum(low_recv[c] for c in range(chips)).astype(BF16).astype(F32)
    spread_low = jnp.concatenate([masks[p] * low_mine for p in range(nodes)], axis=0).astype(BF16)
    grad_b[...] = (
        adapter_scale * jnp.dot(spread_low, cot_all[...], preferred_element_type=F32)
    ).astype(BF16)
    gb_copies = exchange(
        "node",
        nodes,
        me,
        gb_sem,
        lambda q: grad_b.at[rows_of(q, rank_part)],
        got_b.at[rows_of(me, rank_part)],
    )
    start(gb_copies)
    got_b[rows_of(me, rank_part), :] = grad_b[rows_of(me, rank_part), :]
    lora[...] = adapter_scale * lax.dot_general(
        spread_low, recv_b[...], TN, preferred_element_type=F32
    )

    def part_copies(shard):
        copies = []
        cols = rows_of(shard, w_cols)
        for o in range(1, chips):
            peer = lax.rem(chip + o, chips)
            copies.append(
                pltpu.make_async_remote_copy(
                    src_ref=part_send.at[rows_of(peer, out_rows), cols],
                    dst_ref=part_recv.at[chip, :, cols],
                    send_sem=part_send_sem.at[shard, o - 1],
                    recv_sem=part_recv_sem.at[shard, o - 1],
                    device_id={"chip": peer},
                    device_id_type=MESH,
                )
            )
        return copies

    def chunk(shard, weight):
        cols = rows_of(shard, w_cols)

        def body(c, carry):
            rows = rows_of(c, out_rows)
            part_send[rows, cols] = (
                jnp.dot(tokens_ref[rows, :], weight[...], preferred_element_type=F32)
                + lora[rows, cols]
            ).astype(BF16)
            return carry

        lax.fori_loop(0, chips, body, 0)
        start(part_copies(shard))

    loads[4].wait()
    chunk(me, w_all.at[me])
    for j in range(nodes - 1):
        if 1 <= j < nodes - 2:
            w_step(j + 1)
            if j + 1 == nodes - 2:
                start_ga(False)
        for way in (0, 1):
            have, shard = w_from(way, j)

            @pl.when(have)
            def _():
                for o in range(1, groups):
                    theirs = rows_of(lax.rem(group + groups - o, groups), half)
                    pltpu.make_async_remote_copy(
                        src_ref=w_all.at[shard, theirs],
                        dst_ref=w_all.at[shard, theirs],
                        send_sem=wg_send_sem.at[way, j, o - 1],
                        recv_sem=wg_recv_sem.at[way, j, o - 1],
                        device_id={"groups": lax.rem(group + o, groups)},
                        device_id_type=MESH,
                    ).wait_recv()
                chunk(shard, w_all.at[shard])

    landed(ga_copies)
    landed(gb_copies)
    weights = [picks(q) for q in range(nodes)]
    for j in range(owned):
        total_a_ref[j] = sum(
            weights[q][j] * got_a[q * rank : (q + 1) * rank, :].astype(F32) for q in range(nodes)
        )
        total_b_ref[j] = sum(
            weights[q][j] * got_b[q * rank_part : (q + 1) * rank_part, :].astype(F32)
            for q in range(nodes)
        )

    for shard in range(nodes):
        landed(part_copies(shard))
    part_recv[chip] = part_send[rows_of(chip, out_rows), :]
    out_ref[...] = sum(part_recv[c].astype(F32) for c in range(chips)).astype(BF16)

    for copies in (
        info_copies,
        cot_copies,
        b_copies,
        a_copies,
        back_copies,
        ga_copies,
        low_copies,
        gb_copies,
    ):
        for c in copies:
            c.wait_send()
    for shard in range(nodes):
        for c in part_copies(shard):
            c.wait_send()
    for j in range(nodes - 1):
        for way in (0, 1):
            go, copy = w_hop(way, j)

            @pl.when(go)
            def _():
                copy.wait_send()

            have, shard = w_from(way, j)

            @pl.when(have)
            def _():
                for c in w_share(way, j, shard):
                    c.wait_send()


def local_fused(
    nodes,
    chips,
    groups,
    tokens,
    cotangent,
    frozen_value_weight,
    adapter_a,
    adapter_b,
    first_a,
    first_b,
    second_a,
    second_b,
    token_slot,
    adapter_slot,
    request_list,
    request_count,
):
    owned, depth, rank = adapter_a.shape
    rank_part = adapter_b.shape[1]
    rows = tokens.shape[0]
    out_rows, width = cotangent.shape
    w_cols = frozen_value_weight.shape[1]
    vmem = pl.BlockSpec(memory_space=pltpu.VMEM)
    smem = pl.BlockSpec(memory_space=pltpu.SMEM)
    dma = pltpu.SemaphoreType.DMA
    output, total_a, total_b = pl.pallas_call(
        functools.partial(step_kernel, nodes, chips, groups),
        out_shape=(
            jax.ShapeDtypeStruct((out_rows, width), BF16),
            jax.ShapeDtypeStruct((owned, rank, depth), F32),
            jax.ShapeDtypeStruct((owned, rank_part, width), F32),
        ),
        in_specs=[smem] * 3 + [vmem] + [pl.BlockSpec(memory_space=pl.ANY)] * 5,
        out_specs=(vmem, vmem, vmem),
        scratch_shapes=[
            pltpu.VMEM((rows, depth), BF16),
            pltpu.VMEM((owned, rank, depth), BF16),
            pltpu.VMEM((owned, rank_part, width), BF16),
            pltpu.VMEM((nodes, 8, 128), jnp.int32),
            pltpu.VMEM((rows, width), BF16),
            pltpu.VMEM((nodes, depth, w_cols), BF16),
            pltpu.VMEM((nodes * rank, depth), BF16),
            pltpu.VMEM((nodes * rank, depth), BF16),
            pltpu.VMEM((nodes * rank_part, width), BF16),
            pltpu.VMEM((nodes * rank_part, width), BF16),
            pltpu.VMEM((rank, rows), BF16),
            pltpu.VMEM((nodes * rank, depth), BF16),
            pltpu.VMEM((nodes * rank, depth), BF16),
            pltpu.VMEM((nodes * rank_part, width), BF16),
            pltpu.VMEM((nodes * rank_part, width), BF16),
            pltpu.VMEM((nodes * rank, rows), F32),
            pltpu.VMEM((rank, rows), F32),
            pltpu.VMEM((chips, rank_part, rows), F32),
            pltpu.VMEM((rows, width), F32),
            pltpu.VMEM((rows, width), BF16),
            pltpu.VMEM((chips, out_rows, width), BF16),
            dma((2, nodes - 1)),
            dma((2, chips - 1)),
            dma((2, nodes - 1)),
            dma((2, nodes - 1)),
            dma((2, chips - 1)),
            dma((2, chips - 1)),
            dma((2, nodes - 1)),
            dma((2, nodes - 1)),
            dma((2, 2, nodes - 1)),
            dma((2, nodes - 1, groups - 1)),
            dma((2, nodes - 1, groups - 1)),
            dma((nodes, chips - 1)),
            dma((nodes, chips - 1)),
            dma((5,)),
        ],
        compiler_params=pltpu.CompilerParams(
            collective_id=0, has_side_effects=True, vmem_limit_bytes=60 * 1024 * 1024
        ),
        cost_estimate=pl.CostEstimate(
            flops=2 * rows * depth * (width + 2 * nodes * rank),
            bytes_accessed=8 * 1024 * 1024,
            transcendentals=0,
        ),
    )(
        adapter_slot,
        request_list,
        request_count,
        token_slot.reshape(1, rows),
        tokens,
        cotangent,
        frozen_value_weight,
        jnp.swapaxes(adapter_a, 1, 2),
        adapter_b,
    )
    new_a, moment_a, square_a = adam_update(
        adapter_a, first_a, second_a, jnp.swapaxes(total_a, 1, 2)
    )
    new_b, moment_b, square_b = adam_update(adapter_b, first_b, second_b, total_b)
    return (output, new_a, new_b, moment_a, moment_b, square_a, square_b)


def solution(mesh):
    nodes, chips, groups = (mesh.shape[name] for name in ("node", "chip", "groups"))
    fits = 2 <= nodes <= 4 and chips >= 2 and groups >= 2
    local = functools.partial(local_fused, nodes, chips, groups) if fits else local_plain
    return jax.shard_map(
        local,
        mesh=mesh,
        in_specs=(
            P(("groups", "node"), "chip"),
            P(("groups", "node", "chip"), None),
            P("chip", "node"),
            P(("groups", "node"), "chip", None),
            P(("groups", "node"), "chip", None),
            P(("groups", "node"), "chip", None),
            P(("groups", "node"), "chip", None),
            P(("groups", "node"), "chip", None),
            P(("groups", "node"), "chip", None),
            P(("groups", "node")),
            P("groups"),
            P(("groups", "node"), None),
            P(("groups", "node")),
        ),
        out_specs=(
            P(("groups", "node", "chip"), None),
            P(("groups", "node"), "chip", None),
            P(("groups", "node"), "chip", None),
            P(("groups", "node"), "chip", None),
            P(("groups", "node"), "chip", None),
            P(("groups", "node"), "chip", None),
            P(("groups", "node"), "chip", None),
        ),
        check_vma=False,
    )
```

```python
import functools

import jax
import jax.numpy as jnp
from jax import lax
from jax.experimental import pallas as pl
from jax.experimental.pallas import tpu as pltpu
from jax.sharding import PartitionSpec as P

adapter_scale = 2.0
beta_one = 0.9
beta_two = 0.999
rate = 0.001
eps_adam = 1e-08
bias_one = 1.0
bias_two = 0.632304575229036


def adam_update(param, first, second, grad):
    first_new = beta_one * first + (1.0 - beta_one) * grad
    second_new = beta_two * second + (1.0 - beta_two) * grad * grad
    update = first_new / bias_one / (jnp.sqrt(second_new / bias_two) + eps_adam)
    return ((param.astype(jnp.float32) - rate * update).astype(jnp.bfloat16), first_new, second_new)


def local_plain(
    tokens,
    cotangent,
    frozen_value_weight,
    adapter_a,
    adapter_b,
    first_a,
    first_b,
    second_a,
    second_b,
    token_slot,
    adapter_slot,
    request_list,
    request_count,
):
    nodes = lax.axis_size("node")
    this_node = lax.axis_index("node")
    this_chip = lax.axis_index("chip")
    owned = adapter_a.shape[0]
    most = request_list.shape[1]
    rank_part = adapter_b.shape[1]
    width_out = adapter_b.shape[2]
    rows_here = tokens.shape[0]
    positions = jnp.arange(most, dtype=jnp.int32)
    owner_ids = jnp.arange(nodes, dtype=jnp.int32)
    local_ids = jnp.arange(owned, dtype=jnp.int32)
    my_rows = jnp.take(adapter_slot, request_list[0], axis=0)
    my_owner = my_rows // owned
    my_valid = positions < request_count[0]
    all_lists, all_counts = (
        lax.all_gather(request_list, "node", axis=0, tiled=True),
        lax.all_gather(request_count, "node", axis=0, tiled=True),
    )
    all_rows = jnp.take(adapter_slot, all_lists, axis=0)
    hits = (positions[None, :] < all_counts[:, None]) & (all_rows // owned == this_node)
    picks = jnp.sum(
        (hits[:, :, None] & ((all_rows % owned)[:, :, None] == local_ids[None, None, :])).astype(
            jnp.float32
        ),
        axis=1,
    )
    picks_low = picks.astype(jnp.bfloat16)
    send_a = jnp.einsum(
        "pj,jdr->pdr", picks_low, adapter_a, preferred_element_type=jnp.float32
    ).astype(jnp.bfloat16)
    send_b = jnp.einsum(
        "pj,jrv->prv", picks_low, adapter_b, preferred_element_type=jnp.float32
    ).astype(jnp.bfloat16)
    recv_a, recv_b = (
        lax.all_to_all(send_a, "node", split_axis=0, concat_axis=0, tiled=True),
        lax.all_to_all(send_b, "node", split_axis=0, concat_axis=0, tiled=True),
    )
    fetched_a = jnp.take(recv_a, my_owner, axis=0)
    fetched_b = jnp.take(recv_b, my_owner, axis=0)
    onehot = (token_slot[:, None] == positions[None, :]) & my_valid[None, :]
    onehot_f = onehot.astype(jnp.float32)
    onehot_b = onehot.astype(jnp.bfloat16)
    low_part = jnp.einsum("td,kdr->tkr", tokens, fetched_a, preferred_element_type=jnp.float32)
    low_sel = jnp.einsum("tkr,tk->tr", low_part, onehot_f, precision=lax.Precision.HIGHEST)
    low_rank = lax.psum(low_sel, "chip")
    low_bf = low_rank.astype(jnp.bfloat16)
    low_mine = lax.dynamic_slice_in_dim(low_bf, this_chip * rank_part, rank_part, 1)
    spread_rows = (onehot_b[:, :, None] * low_mine[:, None, :]).reshape(rows_here, most * rank_part)
    up_flattened = fetched_b.reshape(most * rank_part, width_out)
    frozen_output = jnp.dot(
        tokens,
        lax.all_gather(frozen_value_weight, "node", axis=1, tiled=True),
        preferred_element_type=jnp.float32,
    )
    partial_terms = frozen_output + adapter_scale * jnp.dot(
        spread_rows, up_flattened, preferred_element_type=jnp.float32
    )
    output = lax.psum_scatter(partial_terms, "chip", scatter_dimension=0, tiled=True).astype(
        jnp.bfloat16
    )
    cot_whole = lax.all_gather(cotangent, "chip", axis=0, tiled=True)
    back_part = jnp.einsum("tv,krv->tkr", cot_whole, fetched_b, preferred_element_type=jnp.float32)
    backward_selected = jnp.einsum(
        "tkr,tk->tr", back_part, onehot_f, precision=lax.Precision.HIGHEST
    )
    backward_half_width = (adapter_scale * backward_selected).astype(jnp.bfloat16)
    back_rank = lax.all_gather(backward_half_width, "chip", axis=1, tiled=True)
    spread_back = onehot_b[:, :, None] * back_rank[:, None, :]
    grad_down = jnp.einsum("td,tkr->kdr", tokens, spread_back, preferred_element_type=jnp.float32)
    up_gradient = adapter_scale * jnp.einsum(
        "tk,tv->kv", spread_rows, cot_whole, preferred_element_type=jnp.float32
    )
    up_gradient = up_gradient.reshape(most, rank_part, width_out)
    route = (my_valid[:, None] & (my_owner[:, None] == owner_ids[None, :])).astype(jnp.float32)
    send_down = jnp.einsum("ko,kdr->odr", route, grad_down, precision=lax.Precision.HIGHEST)
    send_up = jnp.einsum("ko,krv->orv", route, up_gradient, precision=lax.Precision.HIGHEST)
    recv_down, recv_up = (
        lax.all_to_all(
            send_down.astype(jnp.bfloat16), "node", split_axis=0, concat_axis=0, tiled=True
        ).astype(send_down.dtype),
        lax.all_to_all(
            send_up.astype(jnp.bfloat16), "node", split_axis=0, concat_axis=0, tiled=True
        ).astype(send_up.dtype),
    )
    total_down = jnp.einsum("pj,pdr->jdr", picks, recv_down, precision=lax.Precision.HIGHEST)
    total_up = jnp.einsum("pj,prv->jrv", picks, recv_up, precision=lax.Precision.HIGHEST)
    new_a, moment_a, square_a = adam_update(adapter_a, first_a, second_a, total_down)
    new_b, moment_b, square_b = adam_update(adapter_b, first_b, second_b, total_up)
    return (output, new_a, new_b, moment_a, moment_b, square_a, square_b)


MESH = pl.DeviceIdType.MESH
NT = (((1,), (1,)), ((), ()))
TN = (((0,), (0,)), ((), ()))
F32 = jnp.float32
BF16 = jnp.bfloat16


def rows_of(index, size):
    return pl.ds(pl.multiple_of(index * size, size), size)


def step_kernel(
    nodes,
    chips,
    groups,
    slot_ref,
    list_ref,
    count_ref,
    token_slot_ref,
    tokens_in,
    cot_ref,
    w_ref,
    a_in,
    b_in,
    out_ref,
    total_a_ref,
    total_b_ref,
    tokens_ref,
    a_ref,
    b_ref,
    info,
    cot_all,
    w_all,
    send_a,
    recv_a,
    send_b,
    recv_b,
    back_all,
    grad_a,
    got_a,
    grad_b,
    got_b,
    low_all,
    low_send,
    low_recv,
    lora,
    part_send,
    part_recv,
    info_sem,
    cot_sem,
    a_sem,
    b_sem,
    back_sem,
    low_sem,
    ga_sem,
    gb_sem,
    w_sem,
    wg_send_sem,
    wg_recv_sem,
    part_send_sem,
    part_recv_sem,
    local_sem,
):
    me = lax.axis_index("node")
    chip = lax.axis_index("chip")
    group = lax.axis_index("groups")
    owned, rank, depth = a_ref.shape
    rank_part = b_ref.shape[1]
    most = list_ref.shape[1]
    tokens_n = tokens_ref.shape[0]
    out_rows, width = cot_ref.shape
    w_cols = w_ref.shape[1]
    half = depth // groups

    loads = [
        pltpu.make_async_copy(src, dst, local_sem.at[i])
        for i, (src, dst) in enumerate(
            (
                (b_in, b_ref),
                (a_in, a_ref),
                (cot_ref, cot_all.at[rows_of(chip, out_rows)]),
                (tokens_in, tokens_ref),
                (w_ref, w_all.at[me]),
            )
        )
    ]
    for load in loads:
        load.start()
    barrier = pltpu.get_barrier_semaphore()
    for axis, size, here in (("node", nodes, me), ("chip", chips, chip), ("groups", groups, group)):
        for o in range(1, size):
            pl.semaphore_signal(
                barrier, inc=1, device_id={axis: lax.rem(here + o, size)}, device_id_type=MESH
            )

    lane = lax.broadcasted_iota(jnp.int32, (8, 128), 1)
    mine = jnp.full((8, 128), -1, jnp.int32)
    slots = token_slot_ref[...]
    tok_row = jnp.full(slots.shape, -1, jnp.int32)
    for k in range(most):
        row = jnp.where(k < count_ref[0], slot_ref[list_ref[0, k]], -1)
        mine = jnp.where(lane == k, row, mine)
        tok_row = jnp.where(slots == k, row, tok_row)
    info[me] = mine
    masks = [
        jnp.where((tok_row >= p * owned) & (tok_row < (p + 1) * owned), 1.0, 0.0).astype(F32)
        for p in range(nodes)
    ]
    pl.semaphore_wait(barrier, nodes + chips + groups - 3)

    def exchange(axis, size, here, sem, src_of, dst):
        copies = []
        for o in range(1, size):
            peer = lax.rem(here + o, size)
            copies.append(
                pltpu.make_async_remote_copy(
                    src_ref=src_of(peer),
                    dst_ref=dst,
                    send_sem=sem.at[0, o - 1],
                    recv_sem=sem.at[1, o - 1],
                    device_id={axis: peer},
                    device_id_type=MESH,
                )
            )
        return copies

    def start(copies):
        for c in copies:
            c.start()

    def landed(copies):
        for c in copies:
            c.wait_recv()

    info_copies = exchange("node", nodes, me, info_sem, lambda q: info.at[me], info.at[me])
    start(info_copies)
    cot_copies = exchange(
        "chip", chips, chip, cot_sem, lambda q: cot_ref, cot_all.at[rows_of(chip, out_rows)]
    )
    start(cot_copies)

    my_half = rows_of(group, half)

    def w_hop(way, j):
        shard = me - j if way == 0 else me + j
        have = (shard >= 0) if way == 0 else (shard < nodes)
        may = (me < nodes - 1) if way == 0 else (me > 0)
        peer = me + 1 if way == 0 else me - 1
        src = w_ref.at[my_half] if j == 0 else w_all.at[shard, my_half]
        copy = pltpu.make_async_remote_copy(
            src_ref=src,
            dst_ref=w_all.at[shard, my_half],
            send_sem=w_sem.at[0, way, j],
            recv_sem=w_sem.at[1, way, j],
            device_id={"node": peer},
            device_id_type=MESH,
        )
        return have & may, copy

    def w_from(way, j):
        shard = me - 1 - j if way == 0 else me + 1 + j
        have = (shard >= 0) if way == 0 else (shard < nodes)
        return have, shard

    def w_share(way, j, shard):
        copies = []
        for o in range(1, groups):
            copies.append(
                pltpu.make_async_remote_copy(
                    src_ref=w_all.at[shard, my_half],
                    dst_ref=w_all.at[shard, my_half],
                    send_sem=wg_send_sem.at[way, j, o - 1],
                    recv_sem=wg_recv_sem.at[way, j, o - 1],
                    device_id={"groups": lax.rem(group + o, groups)},
                    device_id_type=MESH,
                )
            )
        return copies

    def w_send(way, j):
        go, copy = w_hop(way, j)

        @pl.when(go)
        def _():
            copy.start()

    def w_step(j):
        for way in (0, 1):
            have, shard = w_from(way, j)

            @pl.when(have)
            def _():
                pltpu.make_async_remote_copy(
                    src_ref=w_all.at[shard, my_half],
                    dst_ref=w_all.at[shard, my_half],
                    send_sem=w_sem.at[0, way, j],
                    recv_sem=w_sem.at[1, way, j],
                    device_id={"node": me - 1 if way == 0 else me + 1},
                    device_id_type=MESH,
                ).wait_recv()
                start(w_share(way, j, shard))

            if j + 1 < nodes - 1:
                w_send(way, j + 1)

    w_send(0, 0)
    w_send(1, 0)

    loads[0].wait()
    loads[1].wait()
    landed(info_copies)

    def picks(q):
        found = info[q]
        return [
            jnp.max(jnp.where(found == me * owned + j, 1.0, 0.0).astype(F32)) for j in range(owned)
        ]

    b_copies = exchange(
        "node",
        nodes,
        me,
        b_sem,
        lambda q: send_b.at[rows_of(q, rank_part)],
        recv_b.at[rows_of(me, rank_part)],
    )
    a_copies = exchange(
        "node", nodes, me, a_sem, lambda q: send_a.at[rows_of(q, rank)], recv_a.at[rows_of(me, rank)]
    )
    for o in range(1, nodes + 1):
        q = lax.rem(me + o, nodes)
        pick = picks(q)
        chosen = sum(pick[j] * b_ref[j].astype(F32) for j in range(owned)).astype(BF16)
        if o < nodes:
            send_b[rows_of(q, rank_part), :] = chosen
            b_copies[o - 1].start()
        else:
            recv_b[rows_of(me, rank_part), :] = chosen
    for o in range(1, nodes + 1):
        q = lax.rem(me + o, nodes)
        pick = picks(q)
        chosen = sum(pick[j] * a_ref[j].astype(F32) for j in range(owned)).astype(BF16)
        if o < nodes:
            send_a[rows_of(q, rank), :] = chosen
        else:
            recv_a[rows_of(me, rank), :] = chosen

    loads[2].wait()
    landed(cot_copies)
    landed(b_copies)
    every = lax.dot_general(recv_b[...], cot_all[...], NT, preferred_element_type=F32)
    back = sum(
        masks[p] * every[p * rank_part : (p + 1) * rank_part] for p in range(nodes)
    )
    back_all[rows_of(chip, rank_part), :] = (adapter_scale * back).astype(BF16)
    back_copies = exchange(
        "chip",
        chips,
        chip,
        back_sem,
        lambda q: back_all.at[rows_of(chip, rank_part)],
        back_all.at[rows_of(chip, rank_part)],
    )
    start(back_copies)
    w_step(0)
    start(a_copies)
    landed(back_copies)

    whole_back = back_all[...].astype(F32)
    spread_back = jnp.concatenate([masks[p] * whole_back for p in range(nodes)], axis=0).astype(BF16)
    loads[3].wait()
    tile = min(512, depth)
    for t in range(depth // tile):
        cols = slice(t * tile, (t + 1) * tile)
        grad_a[:, cols] = jnp.dot(
            spread_back, tokens_ref[:, cols], preferred_element_type=F32
        ).astype(BF16)
    ga_copies = exchange(
        "node", nodes, me, ga_sem, lambda q: grad_a.at[rows_of(q, rank)], got_a.at[rows_of(me, rank)]
    )
    got_a[rows_of(me, rank), :] = grad_a[rows_of(me, rank), :]
    if nodes > 2:
        w_step(1)

    landed(a_copies)
    low_all[...] = lax.dot_general(
        recv_a[...], tokens_ref[...], NT, preferred_element_type=F32
    )
    low_send[...] = sum(masks[p] * low_all[p * rank : (p + 1) * rank, :] for p in range(nodes))
    low_copies = exchange(
        "chip",
        chips,
        chip,
        low_sem,
        lambda q: low_send.at[rows_of(q, rank_part)],
        low_recv.at[chip],
    )
    start(low_copies)
    low_recv[chip] = low_send[rows_of(chip, rank_part), :]
    landed(low_copies)
    low_mine = sum(low_recv[c] for c in range(chips)).astype(BF16).astype(F32)
    spread_low = jnp.concatenate([masks[p] * low_mine for p in range(nodes)], axis=0).astype(BF16)
    grad_b[...] = (
        adapter_scale * jnp.dot(spread_low, cot_all[...], preferred_element_type=F32)
    ).astype(BF16)
    gb_copies = exchange(
        "node",
        nodes,
        me,
        gb_sem,
        lambda q: grad_b.at[rows_of(q, rank_part)],
        got_b.at[rows_of(me, rank_part)],
    )
    start(gb_copies)
    got_b[rows_of(me, rank_part), :] = grad_b[rows_of(me, rank_part), :]
    lora[...] = adapter_scale * lax.dot_general(
        spread_low, recv_b[...], TN, preferred_element_type=F32
    )

    def part_copies(shard):
        copies = []
        cols = rows_of(shard, w_cols)
        for o in range(1, chips):
            peer = lax.rem(chip + o, chips)
            copies.append(
                pltpu.make_async_remote_copy(
                    src_ref=part_send.at[rows_of(peer, out_rows), cols],
                    dst_ref=part_recv.at[chip, :, cols],
                    send_sem=part_send_sem.at[shard, o - 1],
                    recv_sem=part_recv_sem.at[shard, o - 1],
                    device_id={"chip": peer},
                    device_id_type=MESH,
                )
            )
        return copies

    def chunk(shard, weight):
        cols = rows_of(shard, w_cols)

        def body(c, carry):
            rows = rows_of(c, out_rows)
            part_send[rows, cols] = (
                jnp.dot(tokens_ref[rows, :], weight[...], preferred_element_type=F32)
                + lora[rows, cols]
            ).astype(BF16)
            return carry

        lax.fori_loop(0, chips, body, 0)
        start(part_copies(shard))

    loads[4].wait()
    chunk(me, w_all.at[me])
    for j in range(nodes - 1):
        if j >= 2:
            w_step(j)
        if j == nodes - 2:
            start(ga_copies)
        for way in (0, 1):
            have, shard = w_from(way, j)

            @pl.when(have)
            def _():
                for o in range(1, groups):
                    theirs = rows_of(lax.rem(group + groups - o, groups), half)
                    pltpu.make_async_remote_copy(
                        src_ref=w_all.at[shard, theirs],
                        dst_ref=w_all.at[shard, theirs],
                        send_sem=wg_send_sem.at[way, j, o - 1],
                        recv_sem=wg_recv_sem.at[way, j, o - 1],
                        device_id={"groups": lax.rem(group + o, groups)},
                        device_id_type=MESH,
                    ).wait_recv()
                chunk(shard, w_all.at[shard])

    landed(ga_copies)
    landed(gb_copies)
    weights = [picks(q) for q in range(nodes)]
    for j in range(owned):
        total_a_ref[j] = sum(
            weights[q][j] * got_a[q * rank : (q + 1) * rank, :].astype(F32) for q in range(nodes)
        )
        total_b_ref[j] = sum(
            weights[q][j] * got_b[q * rank_part : (q + 1) * rank_part, :].astype(F32)
            for q in range(nodes)
        )

    for shard in range(nodes):
        landed(part_copies(shard))
    part_recv[chip] = part_send[rows_of(chip, out_rows), :]
    out_ref[...] = sum(part_recv[c].astype(F32) for c in range(chips)).astype(BF16)

    for copies in (
        info_copies,
        cot_copies,
        b_copies,
        a_copies,
        back_copies,
        ga_copies,
        low_copies,
        gb_copies,
    ):
        for c in copies:
            c.wait_send()
    for shard in range(nodes):
        for c in part_copies(shard):
            c.wait_send()
    for j in range(nodes - 1):
        for way in (0, 1):
            go, copy = w_hop(way, j)

            @pl.when(go)
            def _():
                copy.wait_send()

            have, shard = w_from(way, j)

            @pl.when(have)
            def _():
                for c in w_share(way, j, shard):
                    c.wait_send()


def local_fused(
    nodes,
    chips,
    groups,
    tokens,
    cotangent,
    frozen_value_weight,
    adapter_a,
    adapter_b,
    first_a,
    first_b,
    second_a,
    second_b,
    token_slot,
    adapter_slot,
    request_list,
    request_count,
):
    owned, depth, rank = adapter_a.shape
    rank_part = adapter_b.shape[1]
    rows = tokens.shape[0]
    out_rows, width = cotangent.shape
    w_cols = frozen_value_weight.shape[1]
    vmem = pl.BlockSpec(memory_space=pltpu.VMEM)
    smem = pl.BlockSpec(memory_space=pltpu.SMEM)
    dma = pltpu.SemaphoreType.DMA
    output, total_a, total_b = pl.pallas_call(
        functools.partial(step_kernel, nodes, chips, groups),
        out_shape=(
            jax.ShapeDtypeStruct((out_rows, width), BF16),
            jax.ShapeDtypeStruct((owned, rank, depth), F32),
            jax.ShapeDtypeStruct((owned, rank_part, width), F32),
        ),
        in_specs=[smem] * 3 + [vmem] + [pl.BlockSpec(memory_space=pl.ANY)] * 5,
        out_specs=(vmem, vmem, vmem),
        scratch_shapes=[
            pltpu.VMEM((rows, depth), BF16),
            pltpu.VMEM((owned, rank, depth), BF16),
            pltpu.VMEM((owned, rank_part, width), BF16),
            pltpu.VMEM((nodes, 8, 128), jnp.int32),
            pltpu.VMEM((rows, width), BF16),
            pltpu.VMEM((nodes, depth, w_cols), BF16),
            pltpu.VMEM((nodes * rank, depth), BF16),
            pltpu.VMEM((nodes * rank, depth), BF16),
            pltpu.VMEM((nodes * rank_part, width), BF16),
            pltpu.VMEM((nodes * rank_part, width), BF16),
            pltpu.VMEM((rank, rows), BF16),
            pltpu.VMEM((nodes * rank, depth), BF16),
            pltpu.VMEM((nodes * rank, depth), BF16),
            pltpu.VMEM((nodes * rank_part, width), BF16),
            pltpu.VMEM((nodes * rank_part, width), BF16),
            pltpu.VMEM((nodes * rank, rows), F32),
            pltpu.VMEM((rank, rows), F32),
            pltpu.VMEM((chips, rank_part, rows), F32),
            pltpu.VMEM((rows, width), F32),
            pltpu.VMEM((rows, width), BF16),
            pltpu.VMEM((chips, out_rows, width), BF16),
            dma((2, nodes - 1)),
            dma((2, chips - 1)),
            dma((2, nodes - 1)),
            dma((2, nodes - 1)),
            dma((2, chips - 1)),
            dma((2, chips - 1)),
            dma((2, nodes - 1)),
            dma((2, nodes - 1)),
            dma((2, 2, nodes - 1)),
            dma((2, nodes - 1, groups - 1)),
            dma((2, nodes - 1, groups - 1)),
            dma((nodes, chips - 1)),
            dma((nodes, chips - 1)),
            dma((5,)),
        ],
        compiler_params=pltpu.CompilerParams(
            collective_id=0, has_side_effects=True, vmem_limit_bytes=60 * 1024 * 1024
        ),
        cost_estimate=pl.CostEstimate(
            flops=2 * rows * depth * (width + 2 * nodes * rank),
            bytes_accessed=8 * 1024 * 1024,
            transcendentals=0,
        ),
    )(
        adapter_slot,
        request_list,
        request_count,
        token_slot.reshape(1, rows),
        tokens,
        cotangent,
        frozen_value_weight,
        jnp.swapaxes(adapter_a, 1, 2),
        adapter_b,
    )
    new_a, moment_a, square_a = adam_update(
        adapter_a, first_a, second_a, jnp.swapaxes(total_a, 1, 2)
    )
    new_b, moment_b, square_b = adam_update(adapter_b, first_b, second_b, total_b)
    return (output, new_a, new_b, moment_a, moment_b, square_a, square_b)


def solution(mesh):
    nodes, chips, groups = (mesh.shape[name] for name in ("node", "chip", "groups"))
    fits = 2 <= nodes <= 4 and chips >= 2 and groups >= 2
    local = functools.partial(local_fused, nodes, chips, groups) if fits else local_plain
    return jax.shard_map(
        local,
        mesh=mesh,
        in_specs=(
            P(("groups", "node"), "chip"),
            P(("groups", "node", "chip"), None),
            P("chip", "node"),
            P(("groups", "node"), "chip", None),
            P(("groups", "node"), "chip", None),
            P(("groups", "node"), "chip", None),
            P(("groups", "node"), "chip", None),
            P(("groups", "node"), "chip", None),
            P(("groups", "node"), "chip", None),
            P(("groups", "node")),
            P("groups"),
            P(("groups", "node"), None),
            P(("groups", "node")),
        ),
        out_specs=(
            P(("groups", "node", "chip"), None),
            P(("groups", "node"), "chip", None),
            P(("groups", "node"), "chip", None),
            P(("groups", "node"), "chip", None),
            P(("groups", "node"), "chip", None),
            P(("groups", "node"), "chip", None),
            P(("groups", "node"), "chip", None),
        ),
        check_vma=False,
    )
```
